256 devices in a mesh: exp: 32 (over z_hi, x, y), tp: 8 (over z_lo, core).
Axes of the slice: x: 4, y: 4, z: 8 (z_hi: 2, z_lo: 4; z = z_hi * 4 + z_lo), core: 2. Of those that a mesh axis runs over, the one named last changes fastest.
Arguments:
- tokens: bfloat16 [1536, 6144], P(('exp', 'tp')), may hold values from -6 to 6
- routes: int32 [1536, 4], P(('exp', 'tp')), may hold values from 0 to 15, all different within a row; in each aligned block of 6 rows (0 to 5, 6 to 11, ...) at most 2 rows name the same one
- up_weight: bfloat16 [32, 6144, 2688], P('exp', None, 'tp'), may hold values from -0.078125 to 0.078125
- gate_pre: bfloat16 [32, 512, 2688], P('exp', None, 'tp'), may hold values from -6 to 6
- grad_hidden: bfloat16 [32, 512, 2688], P('exp', None, 'tp'), may hold values from -4 to 4
Outputs:
- grad_tokens: bfloat16 [1536, 6144], P(('exp', 'tp'))
- grad_weight: bfloat16 [32, 6144, 2688], P('exp', None, 'tp')
The draws below stay inside these ranges and needn't reach their ends.
Inputs may be any that keep to these rules, and one draw needn't show every extreme that they name: `routes`: each token names 4 different experts; among the 6 tokens of one device no expert is named more than 2 times, a bound that some block reaches.
All inputs are finite; a program needn't handle non-finite values.
Results may differ from the reference program's by a relative error of at most 0.02.
Values may be sent and summed in bfloat16 or wider, within the bound.
No kernel may reach another device: no remote copies, remote signals or barrier semaphores. Data moves between devices by JAX's collectives and lax.ppermute only.
A program may use at most 128 MiB of HBM per device.

```python
import math
import jax
import jax.numpy as jnp
import numpy as np
from jax import lax

D = 6144
FF = 5376
EXPERTS = 16
TOP = 4
TOK_DEV = 6
SUB = 2
CAP = 2
ROWS_E = 512
TOKENS = 1536
N_EXP = 32
N_TP = 8
DEVICES = 256


def block_scale(own_key, shape, split, smallest, high):
    def one(dim, parts):
        steps = jax.random.uniform(jax.random.fold_in(jax.random.fold_in(own_key, 6), dim), (parts,), jnp.float32, smallest / len(split), high / len(split))
        return jnp.repeat(jnp.exp(steps), shape[dim] // parts).reshape((-1,) + (1,) * (len(shape) - dim - 1))

    level = one(*split[0])
    for cut in split[1:]:
        level = level * one(*cut)
    return level


def routed_block(key, own, number, rows, number_of, top, reach, skew):
    ranking = jax.random.permutation(key, number_of)
    packed, ordinary = portions_of(number_of, rows * top, reach, skew, True), portions_of(number_of, rows * top, reach, skew, False)
    places = jnp.arange(number_of)

    def named(sizes, offset_by):
        used = int((sizes > 0).sum())
        fixed = max(1, used // 4)
        moved = fixed + (places - fixed + offset_by * (used - fixed)) % max(1, number_of - fixed)
        return jnp.zeros((number_of,), jnp.int32).at[ranking[jnp.where(places < fixed, places, moved)]].set(jnp.asarray(sizes, jnp.int32))

    sizes = jnp.where(number % 4 == 0, named(packed, number // 4), named(ordinary, number - number // 4 - 1))
    mixed = jax.random.permutation(jax.random.fold_in(own, 3), number_of)
    giver, receiver = mixed[0:number_of // 2 * 2:2], mixed[1:number_of // 2 * 2:2]
    margin = jnp.minimum(sizes[giver] - 1, reach - sizes[receiver]) // 2
    margin = jnp.where((giver == ranking[0]) | (receiver == ranking[0]) | (sizes[receiver] == 0), 0, jnp.maximum(margin, 0))
    moved = jax.random.randint(jax.random.fold_in(own, 4), (number_of // 2,), 0, 1 << 20) % (margin + 1)
    sizes = sizes.at[giver].add(-moved).at[receiver].add(moved)
    members = jnp.searchsorted(jnp.cumsum(sizes), jnp.arange(rows * top), side="right").astype(jnp.int32)
    table = members.reshape(top, rows).T
    table = table[jax.random.permutation(jax.random.fold_in(own, 1), rows)]
    offset_by = jax.random.randint(jax.random.fold_in(own, 2), (rows, 1), 0, top)
    return jnp.take_along_axis(table, (jnp.arange(top)[None, :] + offset_by) % top, axis=1)


def portions_of(count, total, reach, lean, full):
    weights = [(1 << 20) // math.isqrt(grade ** lean) + 1 for grade in range(1, count + 1)]
    largest = reach if full else min(reach, max(-(-total // count), total * weights[0] // sum(weights)))
    least = 1 if total - largest >= count - 1 else 0
    holding, rest = [largest] + [least] * (count - 1), total - largest - least * (count - 1)
    while rest > 0:
        candidates = [i for i in range(1, count) if holding[i] < largest] or [i for i in range(1, count) if holding[i] < reach]
        whole, left = sum([weights[i] for i in candidates]), rest
        for i in candidates:
            extra = min(reach - holding[i], max(1, left * weights[i] // whole), rest)
            holding[i] = holding[i] + extra
            rest = rest - extra
    return np.array(holding)


def centred(own_key, extent, width, most, cuts=(), kind=jnp.bfloat16):
    values = width * jax.random.normal(own_key, extent, jnp.float32)
    if cuts:
        values = values * block_scale(own_key, extent, cuts, -0.22, 0.18)
    return jnp.clip(values, -most, most).astype(kind)


def setup_inputs(seed: int = 0) -> dict:
    splits = jax.random.split(jax.random.key(seed), 6)
    tokens = centred(splits[0], (TOKENS, D), 1.0, 6.0, ((0, 256),))
    routes_keys = jax.random.split(jax.random.fold_in(splits[1], 1), TOKENS // TOK_DEV)
    routes_turns = jax.random.permutation(jax.random.fold_in(splits[1], 3), TOKENS // TOK_DEV)
    routes = jax.vmap(lambda own, number: routed_block(jax.random.fold_in(splits[1], 2), own, number, TOK_DEV, EXPERTS, TOP, CAP, 1))(routes_keys, routes_turns).reshape((TOKENS, TOP))
    up_weight = centred(splits[2], (N_EXP, D, FF // SUB), D ** -0.5, 0.078125, ((0, 32), (2, 8)))
    gate_pre = centred(splits[3], (N_EXP, ROWS_E, FF // SUB), 1.0, 6.0, ((0, 32), (2, 8)))
    grad_hidden = centred(splits[4], (N_EXP, ROWS_E, FF // SUB), 0.3, 4.0, ((0, 32), (2, 8)))
    return {"tokens": tokens, "routes": routes, "up_weight": up_weight, "gate_pre": gate_pre, "grad_hidden": grad_hidden}


def reference(tokens, routes, up_weight, gate_pre, grad_hidden):
    copies_per = N_EXP // EXPERTS
    slice_width = FF // (copies_per * N_TP)
    blocks = routes.reshape(DEVICES, TOK_DEV, TOP)
    experts_ids = jnp.arange(EXPERTS, dtype=jnp.int32)
    named_by = jnp.sum((blocks[:, :, :, None] == experts_ids[None, None, None, :]).astype(jnp.int32), axis=2)
    before = jnp.cumsum(named_by, axis=1) - named_by
    anchor = jnp.arange(DEVICES, dtype=jnp.int32)[:, None, None]
    slot_of = jnp.where(named_by > 0, anchor * CAP + before, ROWS_E).astype(jnp.int32)
    owner_id = jnp.broadcast_to(jnp.arange(TOKENS, dtype=jnp.int32).reshape(DEVICES, TOK_DEV, 1), named_by.shape)
    column = jnp.broadcast_to(experts_ids[None, None, :], named_by.shape)
    slot_table = jnp.full((EXPERTS, ROWS_E + 1), TOKENS, jnp.int32).at[column, slot_of].set(owner_id)[:, :ROWS_E]
    padded = jnp.concatenate([tokens, jnp.zeros((1, D), tokens.dtype)], axis=0)

    def one_part(gathered, part_no):
        row_index = slot_table[part_no // copies_per]
        expert_rows = padded[row_index]
        scaled = (grad_hidden[part_no].astype(jnp.float32) * jax.nn.silu(gate_pre[part_no].astype(jnp.float32))).astype(jnp.bfloat16)
        grad_part = jnp.dot(expert_rows.T, scaled, preferred_element_type=jnp.float32).astype(jnp.bfloat16)
        summed = jnp.zeros((ROWS_E, D), jnp.float32)
        for portion in range(N_TP):
            hidden_part = scaled[:, portion * slice_width:(portion + 1) * slice_width]
            weight_part = up_weight[part_no][:, portion * slice_width:(portion + 1) * slice_width]
            product = jnp.dot(hidden_part, weight_part.T, preferred_element_type=jnp.float32).astype(jnp.bfloat16)
            product = lax.optimization_barrier(product)
            summed = summed + product.astype(jnp.float32)
        gathered = gathered.at[row_index].add(summed)
        return gathered, grad_part

    gathered, grad_weight = lax.scan(one_part, jnp.zeros((TOKENS + 1, D), jnp.float32), jnp.arange(N_EXP, dtype=jnp.int32))
    return gathered[:TOKENS].astype(jnp.bfloat16), grad_weight
```

```python
import jax
import jax.numpy as jnp
from jax import lax
from jax.sharding import Mesh, PartitionSpec as P

EXPERTS = 16
CAP = 2
FAR = ("zh", "x", "yp")
NEAR = ("yi", "zl", "c")
AXES = FAR + NEAR
SIZES = (2, 4, 2, 2, 4, 2)


def place_table(routes):
    named_by = jnp.sum(
        (routes[:, :, None] == jnp.arange(EXPERTS, dtype=jnp.int32)[None, None, :]).astype(jnp.int32),
        axis=1,
    )
    before = jnp.cumsum(named_by, axis=0) - named_by
    placed = (before[:, :, None] == jnp.arange(CAP, dtype=jnp.int32)[None, None, :]) & (
        named_by[:, :, None] > 0
    )
    return placed.astype(jnp.bfloat16)


def body(tokens, routes, up_weight, gate_pre, grad_hidden):
    weight = up_weight[0]
    width, hidden = weight.shape
    placed = place_table(routes)
    up_grads = (
        grad_hidden[0].astype(jnp.float32) * jax.nn.silu(gate_pre[0].astype(jnp.float32))
    ).astype(jnp.bfloat16)
    up_grads = up_grads.reshape(16, 16, CAP, hidden).transpose(1, 0, 2, 3)
    outgoing = jnp.einsum(
        "tec,td->ecd", placed, tokens, preferred_element_type=jnp.float32
    ).astype(jnp.bfloat16)
    arrived = lax.all_to_all(outgoing, FAR, split_axis=0, concat_axis=0, tiled=True)
    terms = jnp.einsum(
        "gsch,dh->gscd", up_grads, weight, preferred_element_type=jnp.float32
    ).astype(jnp.bfloat16)
    summed = lax.psum_scatter(terms, NEAR, scatter_dimension=0, tiled=False)
    rows = lax.all_gather(arrived, NEAR, axis=0, tiled=False)
    returned = lax.all_to_all(summed, FAR, split_axis=0, concat_axis=0, tiled=True)
    grad_part = jnp.einsum("gscd,gsch->dh", rows, up_grads, preferred_element_type=jnp.float32)
    grad_rows = jnp.einsum("tec,ecd->td", placed, returned, preferred_element_type=jnp.float32)
    return (grad_rows.astype(jnp.bfloat16), grad_part.astype(jnp.bfloat16)[None])


def solution(mesh):
    fine = Mesh(mesh.devices.reshape(SIZES), AXES)
    whole = FAR + NEAR
    part, column = ("zh", "x", "yp", "yi"), ("zl", "c")
    in_specs = (
        P(whole, None),
        P(whole, None),
        P(part, None, column),
        P(part, None, column),
        P(part, None, column),
    )
    out_specs = (P(whole, None), P(part, None, column))
    return jax.shard_map(body, mesh=fine, in_specs=in_specs, out_specs=out_specs, check_vma=False)
```

```python
import jax
import jax.numpy as jnp
from jax import lax
from jax.sharding import Mesh, PartitionSpec as P

EXPERTS = 16
CAP = 2
AXES = ("zh", "x", "yp", "yi", "zl", "c")
SIZES = (2, 4, 2, 2, 4, 2)
PLANE = ("x", "yp", "yi")
RING = ("zh", "zl")
TOK = 6
PAD = 8


def place_table(routes):
    named_by = jnp.sum(
        (routes[..., None] == jnp.arange(EXPERTS, dtype=jnp.int32)).astype(jnp.int32), axis=-2
    )
    tri = jnp.tril(jnp.ones((PAD, PAD), jnp.int32), -1)
    before = jnp.einsum("ij,...je->...ie", tri, named_by)
    return (before[..., None] == jnp.arange(CAP, dtype=jnp.int32)) & (named_by[..., None] > 0)


def swap(value):
    return lax.ppermute(value, "c", [(0, 1), (1, 0)])


def body(tokens, routes, up_weight, gate_pre, grad_hidden):
    zh, zl, core = lax.axis_index("zh"), lax.axis_index("zl"), lax.axis_index("c")
    z = zh * 4 + zl
    weight = up_weight[0]
    width, hidden = weight.shape
    half = width // 2

    up_grads = (
        grad_hidden[0].astype(jnp.float32) * jax.nn.silu(gate_pre[0].astype(jnp.float32))
    ).astype(jnp.bfloat16)
    give = lax.dynamic_slice(weight, ((1 - core) * half, 0), (half, hidden))
    keep = lax.dynamic_slice(weight, (core * half, 0), (half, hidden))
    other_weight = swap(give)
    other_grads = swap(up_grads)
    by_dest = up_grads.reshape(2, 16, 16, hidden).transpose(1, 0, 2, 3).reshape(16, 32, hidden)
    other_by_dest = other_grads.reshape(2, 16, 16, hidden).transpose(1, 0, 2, 3).reshape(16, 32, hidden)
    terms = (
        jnp.einsum("grh,dh->grd", by_dest, keep, preferred_element_type=jnp.float32)
        + jnp.einsum("grh,dh->grd", other_by_dest, other_weight, preferred_element_type=jnp.float32)
    ).astype(jnp.bfloat16)
    came_back = lax.all_to_all(terms, PLANE, split_axis=0, concat_axis=0, tiled=True)

    packed = jnp.concatenate(
        [tokens, jnp.pad(routes.astype(jnp.bfloat16), ((0, 0), (0, 124)))], axis=1
    )
    packed = jnp.pad(packed, ((0, PAD - TOK), (0, 0)))
    ring = [packed]
    for shift in range(1, 8):
        ring.append(lax.ppermute(packed, RING, [(i, (i + shift) % 8) for i in range(8)]))
    ring = jnp.stack(ring)
    ring_tokens = ring[:, :, :width]
    real = (jnp.arange(PAD) < TOK)[None, :, None]
    ring_routes = jnp.where(real, ring[:, :, width : width + 4].astype(jnp.int32), -1)
    place = place_table(ring_routes)
    source = (z - jnp.arange(8, dtype=jnp.int32)) % 8
    at = source[:, None] == jnp.arange(8, dtype=jnp.int32)[None, :]
    mine = lax.dynamic_slice(place, (0, 0, zh * 8, 0), (8, PAD, 8, CAP))
    mine = jnp.repeat(mine, 2, axis=2)
    select = (mine[:, :, :, None, :] & at[:, None, None, :, None]).astype(jnp.bfloat16)
    outgoing = jnp.einsum(
        "ktpzs,ktd->pzsd", select, ring_tokens, preferred_element_type=jnp.float32
    ).astype(jnp.bfloat16).reshape(16, 16, width)
    arrived = lax.all_to_all(outgoing, PLANE, split_axis=0, concat_axis=0, tiled=True)
    other_arrived = swap(arrived)
    by_core = up_grads.reshape(2, 16, 4, 2, CAP, hidden).transpose(3, 1, 0, 2, 4, 5)
    by_core = by_core.reshape(2, 256, hidden)
    mine_rows = lax.dynamic_index_in_dim(by_core, core, 0, keepdims=False)
    other_rows = lax.dynamic_index_in_dim(by_core, 1 - core, 0, keepdims=False)
    grad_part = jnp.einsum(
        "rd,rh->dh", arrived.reshape(256, width), mine_rows, preferred_element_type=jnp.float32
    ) + jnp.einsum(
        "rd,rh->dh", other_arrived.reshape(256, width), other_rows, preferred_element_type=jnp.float32
    )

    both_routes = jnp.stack([ring_routes, swap(ring_routes.astype(jnp.bfloat16)).astype(jnp.int32)])
    both_place = place_table(both_routes)
    both = lax.dynamic_slice(both_place, (0, 0, 0, zh * 8, 0), (2, 8, PAD, 8, CAP))
    both = jnp.repeat(both, 2, axis=3).astype(jnp.bfloat16)
    same = (jnp.arange(2)[:, None] ^ core == jnp.arange(2)[None, :]).astype(jnp.bfloat16)
    gather = jnp.einsum(
        "qktps,kz,qc->zctps", both, at.astype(jnp.bfloat16), same
    )
    eye = jnp.eye(16, dtype=jnp.bfloat16).reshape(8, 2, 8, 2)
    gather = jnp.einsum("zctps,zcyb->zctpybs", gather, eye)
    ring_sums = jnp.einsum(
        "zctpybs,pybsd->zctd",
        gather,
        came_back.reshape(16, 8, 2, CAP, half),
        preferred_element_type=jnp.float32,
    ).astype(jnp.bfloat16)
    ring_parts = lax.all_to_all(
        ring_sums.reshape(8, 2 * PAD, half), RING, split_axis=0, concat_axis=0, tiled=True
    )
    total = jnp.sum(ring_parts.astype(jnp.float32), axis=0).astype(jnp.bfloat16).reshape(2, PAD, half)
    own = lax.dynamic_index_in_dim(total, core, 0, keepdims=False)
    other = swap(lax.dynamic_index_in_dim(total, 1 - core, 0, keepdims=False))
    low, high = jnp.where(core == 0, own, other), jnp.where(core == 0, other, own)
    grad_rows = jnp.concatenate([low, high], axis=1)[:TOK]
    return (grad_rows, grad_part.astype(jnp.bfloat16)[None])


def solution(mesh):
    fine = Mesh(mesh.devices.reshape(SIZES), AXES)
    part, column = AXES[:4], AXES[4:]
    in_specs = (
        P(AXES, None),
        P(AXES, None),
        P(part, None, column),
        P(part, None, column),
        P(part, None, column),
    )
    out_specs = (P(AXES, None), P(part, None, column))
    return jax.shard_map(body, mesh=fine, in_specs=in_specs, out_specs=out_specs, check_vma=False)
```

```python
import functools

import jax
import jax.numpy as jnp
from jax import lax
from jax.experimental import pallas as pl
from jax.experimental.pallas import tpu as pltpu
from jax.sharding import Mesh, PartitionSpec as P

EXPERTS = 16
CAP = 2
AXES = ("zh", "x", "yp", "yi", "zl", "c")
SIZES = (2, 4, 2, 2, 4, 2)
FAR = ("zh", "x", "yp")
PLANE = ("x", "yp", "yi")
RING = ("zh", "zl")
TOK = 6
PAD = 8
CUT = 2048
MIB = 1 << 20
BF, F32, I32 = jnp.bfloat16, jnp.float32, jnp.int32


def params(mib=40):
    return pltpu.CompilerParams(vmem_limit_bytes=mib * MIB)


def iota(shape, dim):
    return lax.broadcasted_iota(I32, shape, dim)


def gate_kernel(gate_ref, grad_ref, ut_ref, u_ref):
    gate = gate_ref[...].astype(F32)
    value = (grad_ref[...].astype(F32) * (gate / (1.0 + jnp.exp(-gate)))).astype(BF)
    ut_ref[...] = value
    u_ref[...] = value.T


def gated(gate_t, grad_t):
    hidden, rows = gate_t.shape
    return pl.pallas_call(
        gate_kernel,
        out_shape=(
            jax.ShapeDtypeStruct((hidden, rows), BF),
            jax.ShapeDtypeStruct((rows, hidden), BF),
        ),
        compiler_params=params(),
        cost_estimate=pl.CostEstimate(flops=10**6, bytes_accessed=1400000, transcendentals=172032),
    )(gate_t, grad_t)


def copy_kernel(core_ref, in_ref, out_ref):
    out_ref[...] = in_ref[...]


def other_half(core, weight_t):
    hidden, width = weight_t.shape
    block = 1024
    steps = width // 2 // block
    return pl.pallas_call(
        copy_kernel,
        grid_spec=pltpu.PrefetchScalarGridSpec(
            num_scalar_prefetch=1,
            grid=(steps,),
            in_specs=[pl.BlockSpec((hidden, block), lambda i, core: (0, (1 - core[0]) * steps + i))],
            out_specs=pl.BlockSpec((hidden, block), lambda i, core: (0, i)),
        ),
        out_shape=jax.ShapeDtypeStruct((hidden, width // 2), BF),
        compiler_params=params(),
        cost_estimate=pl.CostEstimate(flops=0, bytes_accessed=4200000, transcendentals=0),
    )(core, weight_t)


def terms_kernel(core_ref, u_ref, v_ref, w_ref, x_ref, out_ref):
    for zh in range(2):
        rows = pl.ds(zh * 256, 256)
        term = jnp.dot(u_ref[rows, :], w_ref[...], preferred_element_type=F32)
        term += jnp.dot(v_ref[rows, :], x_ref[...], preferred_element_type=F32)
        out_ref[:, zh, :, :] = term.astype(BF).reshape(16, 16, term.shape[1])


def terms_of(core, u, v, weight_t, other_t):
    rows, hidden = u.shape
    half = other_t.shape[1]
    block = 512
    steps = half // block
    return pl.pallas_call(
        terms_kernel,
        grid_spec=pltpu.PrefetchScalarGridSpec(
            num_scalar_prefetch=1,
            grid=(steps,),
            in_specs=[
                pl.BlockSpec((rows, hidden), lambda i, core: (0, 0)),
                pl.BlockSpec((rows, hidden), lambda i, core: (0, 0)),
                pl.BlockSpec((hidden, block), lambda i, core: (0, core[0] * steps + i)),
                pl.BlockSpec((hidden, block), lambda i, core: (0, i)),
            ],
            out_specs=pl.BlockSpec((16, 2, 16, block), lambda i, core: (0, 0, 0, i)),
        ),
        out_shape=jax.ShapeDtypeStruct((16, 2, 16, half), BF),
        compiler_params=params(),
        cost_estimate=pl.CostEstimate(flops=4 * rows * hidden * half, bytes_accessed=8000000, transcendentals=0),
    )(core, u, v, weight_t, other_t)


def named_mask(routes, expert):
    named = jnp.zeros(expert.shape, F32)
    for k in range(4):
        named += jnp.where(routes[:, k : k + 1] == expert, 1.0, 0.0)
    return named


def place_kernel(routes_ref, tokens_ref, out_ref):
    rows = 2 * EXPERTS
    column = iota((PAD, rows), 1)
    named = named_mask(routes_ref[...].astype(F32), (column // 2).astype(F32))
    lower = jnp.where(iota((PAD, PAD), 0) > iota((PAD, PAD), 1), 1.0, 0.0)
    before = jnp.dot(lower, named, preferred_element_type=F32)
    chosen = jnp.where(before == (column % 2).astype(F32), named, 0.0).astype(BF)
    out_ref[...] = lax.dot_general(
        chosen, tokens_ref[...], (((0,), (0,)), ((), ())), preferred_element_type=F32
    ).astype(BF)


def placed_rows(routes, tokens):
    return pl.pallas_call(
        place_kernel,
        out_shape=jax.ShapeDtypeStruct((2 * EXPERTS, tokens.shape[1]), BF),
        compiler_params=params(),
        cost_estimate=pl.CostEstimate(flops=10**6, bytes_accessed=500000, transcendentals=0),
    )(routes, tokens)


def choose_kernel(zh_ref, routes_ref, out_ref):
    shape = (8 * 2 * PAD, 512)
    row, column = iota(shape, 0), iota(shape, 1)
    expert = zh_ref[0] * 8 + column // 64
    named = named_mask(routes_ref[...].astype(F32), expert.astype(F32))
    square = (shape[0], shape[0])
    r, s = iota(square, 0), iota(square, 1)
    lower = jnp.where((r // PAD == s // PAD) & (r > s), 1.0, 0.0)
    before = jnp.dot(lower.astype(BF), named.astype(BF), preferred_element_type=F32)
    fits = (before == (column % 2).astype(F32)) & (row // PAD == (column // 2) % 16)
    out_ref[...] = jnp.where(fits, named, 0.0).astype(BF)


def chooser(zh, routes):
    return pl.pallas_call(
        choose_kernel,
        in_specs=[pl.BlockSpec(memory_space=pltpu.SMEM), pl.BlockSpec(memory_space=pltpu.VMEM)],
        out_shape=jax.ShapeDtypeStruct((8 * 2 * PAD, 512), BF),
        compiler_params=params(),
        cost_estimate=pl.CostEstimate(flops=10**6, bytes_accessed=200000, transcendentals=0),
    )(zh, routes)


def combine_kernel(choice_ref, back_ref, out_ref):
    out_ref[...] = jnp.dot(choice_ref[...], back_ref[...], preferred_element_type=F32).astype(BF)


def combined(choice, back):
    rows, width = back.shape
    block = 1024
    return pl.pallas_call(
        combine_kernel,
        grid=(width // block,),
        in_specs=[
            pl.BlockSpec(choice.shape, lambda i: (0, 0)),
            pl.BlockSpec((rows, block), lambda i: (0, i)),
        ],
        out_specs=pl.BlockSpec((choice.shape[0], block), lambda i: (0, i)),
        out_shape=jax.ShapeDtypeStruct((choice.shape[0], width), BF),
        compiler_params=params(),
        cost_estimate=pl.CostEstimate(flops=2 * 128 * rows * width, bytes_accessed=4000000, transcendentals=0),
    )(choice, back)


def order_kernel(own_ref, ut_ref, first_ref, second_ref):
    own = own_ref[0]
    row, column = iota((512, 512), 0), iota((512, 512), 1)
    origin, slot = (column % 32) // 2 * 32, column % 2
    cc = column // 256
    for ref, yr, k in (
        (first_ref, (column // 32) % 2, (column // 64) % 4),
        (second_ref, (column // 128) % 2, (column // 32) % 4),
    ):
        near = jnp.bitwise_xor(own, yr * 16 + k * 4 + cc * 2)
        move = jnp.where(row == origin + near + slot, 1.0, 0.0).astype(BF)
        ref[...] = jnp.dot(ut_ref[...], move, preferred_element_type=F32).astype(BF)


def ordered(own, ut):
    like = jax.ShapeDtypeStruct(ut.shape, BF)
    return pl.pallas_call(
        order_kernel,
        in_specs=[pl.BlockSpec(memory_space=pltpu.SMEM), pl.BlockSpec(memory_space=pltpu.VMEM)],
        out_shape=(like, like),
        compiler_params=params(),
        cost_estimate=pl.CostEstimate(flops=4 * 336 * 512 * 512, bytes_accessed=1000000, transcendentals=0),
    )(own, ut)


def weight_kernel(count, u_ref, *refs):
    rows = jnp.concatenate([ref[...] for ref in refs[:count]], axis=0)
    refs[-1][...] = jnp.dot(u_ref[...], rows, preferred_element_type=F32).astype(BF)


def weight_grad(u, blocks, width, first, block, base=None):
    hidden = u.shape[0]
    rows, columns = blocks[0].shape
    start = first // block
    specs = [pl.BlockSpec(u.shape, lambda i: (0, 0))]
    specs += [pl.BlockSpec((rows, block), lambda i: (0, i)) for _ in blocks]
    operands = [u, *blocks]
    aliases = {}
    if base is not None:
        specs.append(pl.BlockSpec(memory_space=pl.ANY))
        operands.append(base)
        aliases = {len(operands) - 1: 0}
    return pl.pallas_call(
        functools.partial(weight_kernel, len(blocks)),
        grid=(columns // block,),
        in_specs=specs,
        out_specs=pl.BlockSpec((hidden, block), lambda i: (0, start + i)),
        out_shape=jax.ShapeDtypeStruct((hidden, width), BF),
        input_output_aliases=aliases,
        compiler_params=params(),
        cost_estimate=pl.CostEstimate(
            flops=2 * hidden * 512 * columns, bytes_accessed=2 * (512 + hidden) * columns, transcendentals=0
        ),
    )(*operands)


def swap(value, axis):
    return lax.ppermute(value, axis, [(0, 1), (1, 0)])


def cross(value, mask):
    return lax.ppermute(value, "zl", [(i, i ^ mask) for i in range(4)])


def body(tokens, routes, up_weight, gate_pre, grad_hidden):
    place = {name: lax.axis_index(name).astype(I32) for name in AXES}
    core = place["c"]
    core_arg, zh_arg = core[None], place["zh"][None]
    own_arg = (place["yi"] * 16 + place["zl"] * 4 + core * 2)[None]
    weight_t = jnp.swapaxes(up_weight, 1, 2)[0]
    hidden, width = weight_t.shape
    half = width // 2

    give = other_half(core_arg, weight_t)
    other_t = swap(give, "c")
    ut, u = gated(jnp.swapaxes(gate_pre, 1, 2)[0], jnp.swapaxes(grad_hidden, 1, 2)[0])
    other_u = swap(u, "c")

    route_rows = jnp.pad(routes.astype(BF), ((0, PAD - TOK), (0, 124)), constant_values=-1)
    rows = placed_rows(route_rows, jnp.pad(tokens, ((0, PAD - TOK), (0, 0))))
    far = lax.all_to_all(
        rows.reshape(EXPERTS, CAP, width), FAR, split_axis=0, concat_axis=0, tiled=True
    ).reshape(2 * EXPERTS, width)

    terms = terms_of(core_arg, u, other_u, weight_t, other_t)
    back = lax.all_to_all(
        terms.reshape(16, 32, half), PLANE, split_axis=0, concat_axis=0, tiled=True
    ).reshape(512, half)

    one, two = far[:, :CUT], far[:, CUT:]
    run = jnp.concatenate([two] + [cross(two, k) for k in (1, 2, 3)], axis=0)
    pair = jnp.concatenate([one, swap(one, "yi")], axis=0)
    first = [pair] + [cross(pair, k) for k in (1, 2, 3)]
    second = [run, swap(run, "yi")]
    first += [swap(value, "c") for value in first]
    second += [swap(value, "c") for value in second]
    u_first, u_second = ordered(own_arg, ut)
    grad = weight_grad(u_first, first, width, 0, 1024)
    grad = weight_grad(u_second, second, width, CUT, 1024, grad)

    swapped = swap(route_rows, "c")
    low, high = jnp.where(core == 0, route_rows, swapped), jnp.where(core == 0, swapped, route_rows)
    ring_routes = lax.all_to_all(
        jnp.broadcast_to(jnp.concatenate([low, high], axis=0)[None], (8, 2 * PAD, 128)),
        RING, split_axis=0, concat_axis=0, tiled=True,
    ).reshape(8 * 2 * PAD, 128)
    choice = chooser(zh_arg, ring_routes)
    sums = combined(choice, back)
    parts = lax.all_to_all(
        sums.reshape(8, 2 * PAD, half), RING, split_axis=0, concat_axis=0, tiled=True
    )
    total = jnp.sum(parts.astype(F32), axis=0).astype(BF).reshape(2, PAD, half)
    mine = lax.dynamic_index_in_dim(total, core, 0, keepdims=False)
    other = swap(lax.dynamic_index_in_dim(total, 1 - core, 0, keepdims=False), "c")
    left, right = jnp.where(core == 0, mine, other), jnp.where(core == 0, other, mine)
    grad_rows = jnp.concatenate([left, right], axis=1)[:TOK]
    return (grad_rows, jnp.swapaxes(grad[None], 1, 2))


def solution(mesh):
    fine = Mesh(mesh.devices.reshape(SIZES), AXES)
    part, column = AXES[:4], AXES[4:]
    in_specs = (
        P(AXES, None),
        P(AXES, None),
        P(part, None, column),
        P(part, None, column),
        P(part, None, column),
    )
    out_specs = (P(AXES, None), P(part, None, column))
    return jax.shard_map(body, mesh=fine, in_specs=in_specs, out_specs=out_specs, check_vma=False)
```

```python
import functools

import jax
import jax.numpy as jnp
from jax import lax
from jax.experimental import pallas as pl
from jax.experimental.pallas import tpu as pltpu
from jax.sharding import Mesh, PartitionSpec as P

EXPERTS = 16
CAP = 2
AXES = ("zh", "x", "yp", "yi", "zl", "c")
SIZES = (2, 4, 2, 2, 4, 2)
FAR = ("zh", "x", "yp")
PLANE = ("x", "yp", "yi")
RING = ("zh", "zl")
TOK = 6
PAD = 8
FOLD = 768
EXTRA = 128
MIB = 1 << 20
BF, F32, I32 = jnp.bfloat16, jnp.float32, jnp.int32


def params(mib=24):
    return pltpu.CompilerParams(vmem_limit_bytes=mib * MIB)


def iota(shape, dim):
    return lax.broadcasted_iota(I32, shape, dim)


def gate_kernel(gate_ref, grad_ref, ut_ref, u_ref):
    gate = gate_ref[...].astype(F32)
    value = (grad_ref[...].astype(F32) * (gate / (1.0 + jnp.exp(-gate)))).astype(BF)
    ut_ref[...] = value
    u_ref[...] = value.T


def gated(gate_t, grad_t):
    hidden, rows = gate_t.shape
    return pl.pallas_call(
        gate_kernel,
        out_shape=(
            jax.ShapeDtypeStruct((hidden, rows), BF),
            jax.ShapeDtypeStruct((rows, hidden), BF),
        ),
        compiler_params=params(60),
        cost_estimate=pl.CostEstimate(flops=10**6, bytes_accessed=1400000, transcendentals=172032),
    )(gate_t, grad_t)


def copy_kernel(core_ref, in_ref, out_ref):
    out_ref[...] = in_ref[...]


def other_half(core, weight_t):
    hidden, width = weight_t.shape
    block = 1024
    steps = width // 2 // block
    return pl.pallas_call(
        copy_kernel,
        grid_spec=pltpu.PrefetchScalarGridSpec(
            num_scalar_prefetch=1,
            grid=(steps,),
            in_specs=[pl.BlockSpec((hidden, block), lambda i, core: (0, (1 - core[0]) * steps + i))],
            out_specs=pl.BlockSpec((hidden, block), lambda i, core: (0, i)),
        ),
        out_shape=jax.ShapeDtypeStruct((hidden, width // 2), BF),
        compiler_params=params(60),
        cost_estimate=pl.CostEstimate(flops=0, bytes_accessed=4200000, transcendentals=0),
    )(core, weight_t)


def terms_kernel(core_ref, u_ref, v_ref, w_ref, x_ref, out_ref):
    term = jnp.dot(u_ref[...], w_ref[...], preferred_element_type=F32)
    term += jnp.dot(v_ref[...], x_ref[...], preferred_element_type=F32)
    term = term.astype(BF).reshape(2, 16, 16, term.shape[1])
    out_ref[:, 0, :, :] = term[0]
    out_ref[:, 1, :, :] = term[1]


def terms_of(core, u, v, weight_t, other_t):
    rows, hidden = u.shape
    half = other_t.shape[1]
    block = 512
    steps = half // block
    return pl.pallas_call(
        terms_kernel,
        grid_spec=pltpu.PrefetchScalarGridSpec(
            num_scalar_prefetch=1,
            grid=(steps,),
            in_specs=[
                pl.BlockSpec((rows, hidden), lambda i, core: (0, 0)),
                pl.BlockSpec((rows, hidden), lambda i, core: (0, 0)),
                pl.BlockSpec((hidden, block), lambda i, core: (0, core[0] * steps + i)),
                pl.BlockSpec((hidden, block), lambda i, core: (0, i)),
            ],
            out_specs=pl.BlockSpec((16, 2, 16, block), lambda i, core: (0, 0, 0, i)),
        ),
        out_shape=jax.ShapeDtypeStruct((16, 2, 16, half), BF),
        compiler_params=params(),
        cost_estimate=pl.CostEstimate(flops=4 * rows * hidden * half, bytes_accessed=8000000, transcendentals=0),
    )(core, u, v, weight_t, other_t)


def named_mask(routes, expert):
    named = jnp.zeros(expert.shape, F32)
    for k in range(4):
        named += jnp.where(routes[:, k : k + 1] == expert, 1.0, 0.0)
    return named


def place_kernel(tokens_ref, routes_ref, out_ref, held_ref, named_ref):
    count, width = tokens_ref.shape
    held_ref[...] = jnp.zeros(held_ref.shape, F32)
    held_ref[:count, :] = tokens_ref[...].astype(F32)
    named_ref[...] = jnp.full(named_ref.shape, -1.0, F32)
    named_ref[:count, :4] = routes_ref[...].astype(F32).T
    routes = named_ref[...]
    column = iota((PAD, 256), 1)
    named = named_mask(routes, (column // 16).astype(F32))
    lower = jnp.where(iota((PAD, PAD), 0) > iota((PAD, PAD), 1), 1.0, 0.0)
    before = jnp.dot(lower, named, preferred_element_type=F32)
    chosen = jnp.where(before == (column // 8 % 2).astype(F32), named, 0.0)
    total = jnp.zeros((256, FOLD), F32)
    for fold in range(width // FOLD):
        pick = jnp.where(column % 8 == fold, chosen, 0.0).T.astype(BF)
        piece = held_ref[:, fold * FOLD : fold * FOLD + FOLD].astype(BF)
        total += jnp.dot(pick, piece, preferred_element_type=F32)
    out_ref[:, :FOLD] = total.astype(BF)
    spread = jnp.where(iota((256, PAD), 0) % PAD == iota((256, PAD), 1), 1.0, 0.0).astype(BF)
    out_ref[:, FOLD:] = jnp.dot(spread, routes.astype(BF), preferred_element_type=F32).astype(BF)


def placed_rows(tokens, routes):
    return pl.pallas_call(
        place_kernel,
        out_shape=jax.ShapeDtypeStruct((256, FOLD + EXTRA), BF),
        scratch_shapes=[pltpu.VMEM((PAD, tokens.shape[1]), F32), pltpu.VMEM((PAD, EXTRA), F32)],
        compiler_params=params(60),
        cost_estimate=pl.CostEstimate(flops=10**6, bytes_accessed=500000, transcendentals=0),
    )(tokens, routes)


def unfold_kernel(at_ref, rows_ref, out_ref):
    width = out_ref.shape[1] - EXTRA
    rows = rows_ref[...]
    r, s = iota((32, 256), 0), iota((32, 256), 1)
    for fold in range(width // FOLD):
        move = jnp.where(s == r * 8 + fold, 1.0, 0.0).astype(BF)
        piece = jnp.dot(move, rows[:, :FOLD], preferred_element_type=F32)
        out_ref[:, fold * FOLD : fold * FOLD + FOLD] = piece.astype(BF)
    move = jnp.where((s == r // 8 * 128 + at_ref[0] * 16 + r % 8) & (r < 16), 1.0, 0.0).astype(BF)
    out_ref[:, width:] = jnp.dot(move, rows[:, FOLD:], preferred_element_type=F32).astype(BF)


def unfold(at, rows, width):
    return pl.pallas_call(
        unfold_kernel,
        in_specs=[pl.BlockSpec(memory_space=pltpu.SMEM), pl.BlockSpec(memory_space=pltpu.VMEM)],
        out_shape=jax.ShapeDtypeStruct((32, width + EXTRA), BF),
        compiler_params=params(),
        cost_estimate=pl.CostEstimate(flops=10**6, bytes_accessed=1000000, transcendentals=0),
    )(at, rows)


def choose_kernel(at_ref, mine_ref, other_ref, out_ref):
    shape = (8 * 2 * PAD, 512)
    row, column = iota(shape, 0), iota(shape, 1)
    expert = at_ref[0] * 8 + column // 64
    routes = jnp.concatenate([mine_ref[...], other_ref[...]], axis=0)
    r, s = iota((128, 256), 0), iota((128, 256), 1)
    came = (r // 8) % 2 * 128 + jnp.bitwise_xor((r // 16) % 4, at_ref[1]) * 32 + r // 64 * 8 + r % 8
    move = jnp.where(came == s, 1.0, 0.0).astype(BF)
    named = named_mask(jnp.dot(move, routes, preferred_element_type=F32), expert.astype(F32))
    r, s = iota((128, 128), 0), iota((128, 128), 1)
    lower = jnp.where((r // PAD == s // PAD) & (r > s), 1.0, 0.0)
    before = jnp.dot(lower.astype(BF), named.astype(BF), preferred_element_type=F32)
    device = row // 16 * 2 + jnp.bitwise_xor((row // 8) % 2, at_ref[2])
    fits = (before == (column % 2).astype(F32)) & (device == (column // 2) % 16)
    out_ref[...] = jnp.where(fits, named, 0.0).astype(BF)


def chooser(at, mine, other):
    return pl.pallas_call(
        choose_kernel,
        in_specs=[pl.BlockSpec(memory_space=pltpu.SMEM)] + [pl.BlockSpec(memory_space=pltpu.VMEM)] * 2,
        out_shape=jax.ShapeDtypeStruct((8 * 2 * PAD, 512), BF),
        compiler_params=params(),
        cost_estimate=pl.CostEstimate(flops=10**6, bytes_accessed=200000, transcendentals=0),
    )(at, mine, other)


def combine_kernel(choice_ref, back_ref, out_ref):
    out_ref[...] = jnp.dot(choice_ref[...], back_ref[...], preferred_element_type=F32).astype(BF)


def combined(choice, back):
    rows, width = back.shape
    block = 1024
    return pl.pallas_call(
        combine_kernel,
        grid=(width // block,),
        in_specs=[
            pl.BlockSpec(choice.shape, lambda i: (0, 0)),
            pl.BlockSpec((rows, block), lambda i: (0, i)),
        ],
        out_specs=pl.BlockSpec((choice.shape[0], block), lambda i: (0, i)),
        out_shape=jax.ShapeDtypeStruct((choice.shape[0], width), BF),
        compiler_params=params(),
        cost_estimate=pl.CostEstimate(flops=2 * 128 * rows * width, bytes_accessed=4000000, transcendentals=0),
    )(choice, back)


def order_kernel(own_ref, ut_ref, out_ref):
    row, column = iota((512, 512), 0), iota((512, 512), 1)
    near = (column // 128) % 2 * 16 + (column // 32) % 4 * 4 + column // 256 * 2
    origin = column % 32 // 2 * 32 + jnp.bitwise_xor(own_ref[0], near) + column % 2
    move = jnp.where(row == origin, 1.0, 0.0).astype(BF)
    out_ref[...] = jnp.dot(ut_ref[...], move, preferred_element_type=F32).astype(BF)


def ordered(own, ut):
    return pl.pallas_call(
        order_kernel,
        in_specs=[pl.BlockSpec(memory_space=pltpu.SMEM), pl.BlockSpec(memory_space=pltpu.VMEM)],
        out_shape=jax.ShapeDtypeStruct(ut.shape, BF),
        compiler_params=params(),
        cost_estimate=pl.CostEstimate(flops=2 * 336 * 512 * 512, bytes_accessed=1000000, transcendentals=0),
    )(own, ut)


def weight_kernel(count, u_ref, *refs):
    rows = jnp.concatenate([ref[...] for ref in refs[:count]], axis=0)
    refs[-1][...] = jnp.dot(u_ref[...], rows, preferred_element_type=F32).astype(BF)


def weight_grad(u, blocks, width, first, columns, block, base=None):
    hidden = u.shape[0]
    rows = blocks[0][0].shape[0]
    start = first // block
    specs = [pl.BlockSpec(u.shape, lambda i: (0, 0))]
    for _, at in blocks:
        specs.append(pl.BlockSpec((rows, block), lambda i, at=at: (0, at // block + i)))
    operands = [u, *[value for value, _ in blocks]]
    aliases = {}
    if base is not None:
        specs.append(pl.BlockSpec(memory_space=pl.ANY))
        operands.append(base)
        aliases = {len(operands) - 1: 0}
    return pl.pallas_call(
        functools.partial(weight_kernel, len(blocks)),
        grid=(columns // block,),
        in_specs=specs,
        out_specs=pl.BlockSpec((hidden, block), lambda i: (0, start + i)),
        out_shape=jax.ShapeDtypeStruct((hidden, width), BF),
        input_output_aliases=aliases,
        compiler_params=params(),
        cost_estimate=pl.CostEstimate(
            flops=2 * hidden * 512 * columns, bytes_accessed=2 * (512 + hidden) * columns, transcendentals=0
        ),
    )(*operands)


def swap(value, axis):
    return lax.ppermute(value, axis, [(0, 1), (1, 0)])


def cross(value, mask):
    return lax.ppermute(value, "zl", [(i, i ^ mask) for i in range(4)])


def body(tokens, routes, up_weight, gate_pre, grad_hidden):
    place = {name: lax.axis_index(name).astype(I32) for name in AXES}
    core, zh, zl, yi = place["c"], place["zh"], place["zl"], place["yi"]
    own_arg = (yi * 16 + zl * 4 + core * 2)[None]
    at_arg = jnp.stack([zh, zl, core])
    home_arg = (place["x"] * 2 + place["yp"])[None]
    weight_t = jnp.swapaxes(up_weight, 1, 2)[0]
    hidden, width = weight_t.shape
    half = width // 2

    rows = placed_rows(tokens, routes.T)
    rows, weight_t = lax.optimization_barrier((rows, weight_t))
    arrived = lax.all_to_all(
        rows.reshape(16, 16, FOLD + EXTRA), FAR, split_axis=0, concat_axis=0, tiled=True
    ).reshape(256, FOLD + EXTRA)

    give = other_half(core[None], weight_t)
    other_t = swap(give, "c")
    ut, u = gated(jnp.swapaxes(gate_pre, 1, 2)[0], jnp.swapaxes(grad_hidden, 1, 2)[0])
    other_u = swap(u, "c")
    terms = terms_of(core[None], u, other_u, weight_t, other_t)
    back = lax.all_to_all(
        terms.reshape(16, 32, half), PLANE, split_axis=0, concat_axis=0, tiled=True
    ).reshape(512, half)

    two = unfold(home_arg, arrived, width)
    run = jnp.concatenate([two] + [cross(two, k) for k in (1, 2, 3)], axis=0)
    pairs = [swap(run[:, :half], "yi"), swap(run[:, half:width], "yi")]
    u_rows = ordered(own_arg, ut)
    run_routes = run[:, width:]
    choice = chooser(at_arg, run_routes, swap(run_routes, "c"))
    other_run = swap(run, "c")

    sums = combined(choice, back)
    parts = lax.all_to_all(
        sums.reshape(8, 2 * PAD, half), RING, split_axis=0, concat_axis=0, tiled=True
    )
    total = jnp.sum(parts.astype(F32), axis=0).astype(BF)
    mine, other = total[:PAD], swap(total[PAD:], "c")
    left, right = jnp.where(core == 0, mine, other), jnp.where(core == 0, other, mine)
    grad_rows = jnp.concatenate([left, right], axis=1)[:TOK]

    def part(index, pair, base):
        at = index * half
        rows = [(run, at), (pair, 0), (other_run, at), (swap(pair, "c"), 0)]
        return weight_grad(u_rows, rows, width, at, half, 1024, base)

    grad = part(0, lax.optimization_barrier((pairs[0], sums))[0], None)
    pair, grad = lax.optimization_barrier((pairs[1], grad))
    grad = part(1, pair, grad)
    return (grad_rows, jnp.swapaxes(grad[None], 1, 2))


def solution(mesh):
    fine = Mesh(mesh.devices.reshape(SIZES), AXES)
    part, column = AXES[:4], AXES[4:]
    in_specs = (
        P(AXES, None),
        P(AXES, None),
        P(part, None, column),
        P(part, None, column),
        P(part, None, column),
    )
    out_specs = (P(AXES, None), P(part, None, column))
    return jax.shard_map(body, mesh=fine, in_specs=in_specs, out_specs=out_specs, check_vma=False)
```

```python
import functools

import jax
import jax.numpy as jnp
from jax import lax
from jax.experimental import pallas as pl
from jax.experimental.pallas import tpu as pltpu
from jax.sharding import Mesh, PartitionSpec as P

EXPERTS = 16
CAP = 2
AXES = ("zh", "x", "yp", "yi", "zl", "c")
SIZES = (2, 4, 2, 2, 4, 2)
FAR = ("zh", "x", "yp")
PLANE = ("x", "yp", "yi")
RING = ("zh", "zl")
TOK = 6
PAD = 8
FOLD = 768
EXTRA = 128
MIB = 1 << 20
SMALL = pl.CostEstimate(flops=1000, bytes_accessed=1000, transcendentals=0)
BF, F32, I32 = jnp.bfloat16, jnp.float32, jnp.int32


def params(mib=24):
    return pltpu.CompilerParams(vmem_limit_bytes=mib * MIB)


def iota(shape, dim):
    return lax.broadcasted_iota(I32, shape, dim)


def gate_kernel(gate_ref, grad_ref, ut_ref, u_ref):
    gate = gate_ref[...].astype(F32)
    value = (grad_ref[...].astype(F32) * (gate / (1.0 + jnp.exp(-gate)))).astype(BF)
    ut_ref[...] = value
    u_ref[...] = value.T


def gated(gate_t, grad_t):
    hidden, rows = gate_t.shape
    return pl.pallas_call(
        gate_kernel,
        out_shape=(
            jax.ShapeDtypeStruct((hidden, rows), BF),
            jax.ShapeDtypeStruct((rows, hidden), BF),
        ),
        compiler_params=params(60),
        cost_estimate=pl.CostEstimate(flops=10**6, bytes_accessed=1400000, transcendentals=172032),
    )(gate_t, grad_t)


def copy_kernel(core_ref, in_ref, out_ref):
    out_ref[...] = in_ref[...]


def other_half(core, weight_t):
    hidden, width = weight_t.shape
    block = 1024
    steps = width // 2 // block
    return pl.pallas_call(
        copy_kernel,
        grid_spec=pltpu.PrefetchScalarGridSpec(
            num_scalar_prefetch=1,
            grid=(steps,),
            in_specs=[pl.BlockSpec((hidden, block), lambda i, core: (0, (1 - core[0]) * steps + i))],
            out_specs=pl.BlockSpec((hidden, block), lambda i, core: (0, i)),
        ),
        out_shape=jax.ShapeDtypeStruct((hidden, width // 2), BF),
        compiler_params=params(60),
        cost_estimate=pl.CostEstimate(flops=0, bytes_accessed=4200000, transcendentals=0),
    )(core, weight_t)


def terms_kernel(core_ref, u_ref, v_ref, w_ref, x_ref, out_ref):
    term = jnp.dot(u_ref[...], w_ref[...], preferred_element_type=F32)
    term += jnp.dot(v_ref[...], x_ref[...], preferred_element_type=F32)
    term = term.astype(BF).reshape(2, 16, 16, term.shape[1])
    out_ref[:, 0, :, :] = term[0]
    out_ref[:, 1, :, :] = term[1]


def terms_of(core, u, v, weight_t, other_t):
    rows, hidden = u.shape
    half = other_t.shape[1]
    block = 1024
    steps = half // block
    return pl.pallas_call(
        terms_kernel,
        grid_spec=pltpu.PrefetchScalarGridSpec(
            num_scalar_prefetch=1,
            grid=(steps,),
            in_specs=[
                pl.BlockSpec((rows, hidden), lambda i, core: (0, 0)),
                pl.BlockSpec((rows, hidden), lambda i, core: (0, 0)),
                pl.BlockSpec((hidden, block), lambda i, core: (0, core[0] * steps + i)),
                pl.BlockSpec((hidden, block), lambda i, core: (0, i)),
            ],
            out_specs=pl.BlockSpec((16, 2, 16, block), lambda i, core: (0, 0, 0, i)),
        ),
        out_shape=jax.ShapeDtypeStruct((16, 2, 16, half), BF),
        compiler_params=params(),
        cost_estimate=pl.CostEstimate(flops=4 * rows * hidden * half, bytes_accessed=8000000, transcendentals=0),
    )(core, u, v, weight_t, other_t)


def named_mask(routes, expert):
    named = jnp.zeros(expert.shape, F32)
    for k in range(4):
        named += jnp.where(routes[:, k : k + 1] == expert, 1.0, 0.0)
    return named


def place_kernel(tokens_ref, routes_ref, out_ref, held_ref, named_ref):
    count, width = tokens_ref.shape
    held_ref[...] = jnp.zeros(held_ref.shape, F32)
    held_ref[:count, :] = tokens_ref[...].astype(F32)
    named_ref[...] = jnp.full(named_ref.shape, -1.0, F32)
    named_ref[:count, :4] = routes_ref[...].astype(F32).T
    routes = named_ref[...]
    column = iota((PAD, 256), 1)
    named = named_mask(routes, (column // 16).astype(F32))
    lower = jnp.where(iota((PAD, PAD), 0) > iota((PAD, PAD), 1), 1.0, 0.0)
    before = jnp.dot(lower, named, preferred_element_type=F32)
    chosen = jnp.where(before == (column // 8 % 2).astype(F32), named, 0.0)
    folds = range(width // FOLD)
    pick = jnp.concatenate([jnp.where(column % 8 == fold, chosen, 0.0) for fold in folds], axis=0)
    pieces = [held_ref[:, fold * FOLD : fold * FOLD + FOLD] for fold in folds]
    pieces = jnp.concatenate(pieces, axis=0).astype(BF)
    total = jnp.dot(pick.T.astype(BF), pieces, preferred_element_type=F32)
    out_ref[:, :FOLD] = total.astype(BF)
    spread = jnp.where(iota((256, PAD), 0) % PAD == iota((256, PAD), 1), 1.0, 0.0).astype(BF)
    out_ref[:, FOLD:] = jnp.dot(spread, routes.astype(BF), preferred_element_type=F32).astype(BF)


def placed_rows(tokens, routes):
    return pl.pallas_call(
        place_kernel,
        out_shape=jax.ShapeDtypeStruct((256, FOLD + EXTRA), BF),
        scratch_shapes=[pltpu.VMEM((PAD, tokens.shape[1]), F32), pltpu.VMEM((PAD, EXTRA), F32)],
        compiler_params=params(60),
        cost_estimate=pl.CostEstimate(flops=10**6, bytes_accessed=500000, transcendentals=0),
    )(tokens, routes)


def unfold_kernel(at_ref, rows_ref, out_ref):
    width = out_ref.shape[1] - EXTRA
    rows = rows_ref[...]
    r, s = iota((32, 256), 0), iota((32, 256), 1)
    for fold in range(width // FOLD):
        move = jnp.where(s == r * 8 + fold, 1.0, 0.0).astype(BF)
        piece = jnp.dot(move, rows[:, :FOLD], preferred_element_type=F32)
        out_ref[:, fold * FOLD : fold * FOLD + FOLD] = piece.astype(BF)
    move = jnp.where((s == r // 8 * 128 + at_ref[0] * 16 + r % 8) & (r < 16), 1.0, 0.0).astype(BF)
    out_ref[:, width:] = jnp.dot(move, rows[:, FOLD:], preferred_element_type=F32).astype(BF)


def unfold(at, rows, width):
    return pl.pallas_call(
        unfold_kernel,
        in_specs=[pl.BlockSpec(memory_space=pltpu.SMEM), pl.BlockSpec(memory_space=pltpu.VMEM)],
        out_shape=jax.ShapeDtypeStruct((32, width + EXTRA), BF),
        compiler_params=params(),
        cost_estimate=pl.CostEstimate(flops=10**6, bytes_accessed=1000000, transcendentals=0),
    )(at, rows)


def choose_kernel(at_ref, *refs):
    out_ref = refs[-1]
    shape = (8 * 2 * PAD, 512)
    row, column = iota(shape, 0), iota(shape, 1)
    expert = at_ref[0] * 8 + column // 64
    routes = jnp.concatenate([ref[...] for ref in refs[:-1]], axis=0)
    r, s = iota((128, 256), 0), iota((128, 256), 1)
    came = (r // 8) % 2 * 128 + jnp.bitwise_xor((r // 16) % 4, at_ref[1]) * 32 + r // 64 * 8 + r % 8
    move = jnp.where(came == s, 1.0, 0.0).astype(BF)
    named = named_mask(jnp.dot(move, routes, preferred_element_type=F32), expert.astype(F32))
    r, s = iota((128, 128), 0), iota((128, 128), 1)
    lower = jnp.where((r // PAD == s // PAD) & (r > s), 1.0, 0.0)
    before = jnp.dot(lower.astype(BF), named.astype(BF), preferred_element_type=F32)
    device = row // 16 * 2 + jnp.bitwise_xor((row // 8) % 2, at_ref[2])
    fits = (before == (column % 2).astype(F32)) & (device == (column // 2) % 16)
    chosen = jnp.where(fits, named, 0.0).astype(BF)
    r, s = iota((192, 128), 0), iota((192, 128), 1)
    late = r // 64
    token = r % 8 + jnp.where(late == 0, 0, 12 - 4 * late)
    real = (late == 0) | ((token >= 8) & (token < 12))
    place = r % 64 // 8 * 16 + token // TOK * PAD + token % TOK
    move = jnp.where((place == s) & real, 1.0, 0.0).astype(BF)
    out_ref[...] = jnp.dot(move, chosen, preferred_element_type=F32).astype(BF)


def chooser(at, *runs):
    last = runs[0].shape[1] // EXTRA - 1
    return pl.pallas_call(
        choose_kernel,
        grid=(1,),
        in_specs=[pl.BlockSpec(memory_space=pltpu.SMEM)]
        + [pl.BlockSpec((value.shape[0], EXTRA), lambda i: (0, last)) for value in runs],
        out_specs=pl.BlockSpec((192, 512), lambda i: (0, 0)),
        out_shape=jax.ShapeDtypeStruct((192, 512), BF),
        compiler_params=params(),
        cost_estimate=pl.CostEstimate(flops=10**6, bytes_accessed=200000, transcendentals=0),
    )(at, *runs)


def combine_kernel(choice_ref, back_ref, out_ref):
    half = back_ref.shape[1]
    step = half // 4
    for at in range(0, half // 2, step):
        low = jnp.dot(choice_ref[...], back_ref[:, at : at + step], preferred_element_type=F32)
        high = back_ref[:, half // 2 + at : half // 2 + at + step]
        high = jnp.dot(choice_ref[...], high, preferred_element_type=F32)
        out_ref[:, at : at + step] = low[:64].astype(BF)
        out_ref[:, half // 2 + at : half // 2 + at + step] = high[:64].astype(BF)
        out_ref[:, half + at : half + at + step] = (low[64:128] + high[128:]).astype(BF)


def combined(choice, back):
    rows, half = back.shape
    return pl.pallas_call(
        combine_kernel,
        out_shape=jax.ShapeDtypeStruct((64, half + half // 2), BF),
        compiler_params=params(),
        cost_estimate=pl.CostEstimate(flops=2 * 192 * rows * half, bytes_accessed=4000000, transcendentals=0),
    )(choice, back)


def total_kernel(parts_ref, mine_ref, other_ref):
    half = mine_ref.shape[1]
    total = parts_ref[0].astype(F32)
    for source in range(1, parts_ref.shape[0]):
        total += parts_ref[source].astype(F32)
    total = total.astype(BF)
    mine_ref[...] = total[:, :half]
    r, s = iota((PAD, PAD), 0), iota((PAD, PAD), 1)

    def moved(shift, keep, value):
        move = jnp.where((s == r + shift) & keep, 1.0, 0.0).astype(BF)
        return jnp.dot(move, value, preferred_element_type=F32)

    first = moved(TOK, r < 2, total[:, :half])
    second = (r >= 2) & (r < TOK)
    rest = total[:, half:]
    rest = jnp.concatenate([moved(-2, second, rest), moved(2, second, rest)], axis=1)
    other_ref[...] = (first + rest).astype(BF)


def totalled(parts):
    half = parts.shape[2] * 2 // 3
    like = jax.ShapeDtypeStruct((PAD, half), BF)
    return pl.pallas_call(
        total_kernel,
        out_shape=(like, like),
        compiler_params=params(),
        cost_estimate=SMALL,
    )(parts)


def order_kernel(own_ref, ut_ref, out_ref):
    row, column = iota((512, 512), 0), iota((512, 512), 1)
    near = (column // 128) % 2 * 16 + (column // 32) % 4 * 4 + column // 256 * 2
    origin = column % 32 // 2 * 32 + jnp.bitwise_xor(own_ref[0], near) + column % 2
    move = jnp.where(row == origin, 1.0, 0.0).astype(BF)
    out_ref[...] = jnp.dot(ut_ref[...], move, preferred_element_type=F32).astype(BF)


def ordered(own, ut):
    return pl.pallas_call(
        order_kernel,
        in_specs=[pl.BlockSpec(memory_space=pltpu.SMEM), pl.BlockSpec(memory_space=pltpu.VMEM)],
        out_shape=jax.ShapeDtypeStruct(ut.shape, BF),
        compiler_params=params(),
        cost_estimate=SMALL,
    )(own, ut)


def weight_kernel(count, u_ref, *refs):
    rows = jnp.concatenate([ref[...] for ref in refs[:count]], axis=0)
    refs[-1][...] = jnp.dot(u_ref[...], rows, preferred_element_type=F32).astype(BF)


def weight_grad(u, blocks, width, block):
    hidden = u.shape[0]
    specs = [pl.BlockSpec(u.shape, lambda i: (0, 0))]
    specs += [pl.BlockSpec((value.shape[0], block), lambda i: (0, i)) for value in blocks]
    return pl.pallas_call(
        functools.partial(weight_kernel, len(blocks)),
        grid=(width // block,),
        in_specs=specs,
        out_specs=pl.BlockSpec((hidden, block), lambda i: (0, i)),
        out_shape=jax.ShapeDtypeStruct((hidden, width), BF),
        compiler_params=params(),
        cost_estimate=pl.CostEstimate(
            flops=2 * hidden * 512 * width, bytes_accessed=2 * (512 + hidden) * width, transcendentals=0
        ),
    )(u, *blocks)


def swap(value, axis):
    return lax.ppermute(value, axis, [(0, 1), (1, 0)])


def cross(value, mask):
    return lax.ppermute(value, "zl", [(i, i ^ mask) for i in range(4)])


def body(tokens, routes, up_weight, gate_pre, grad_hidden):
    place = {name: lax.axis_index(name).astype(I32) for name in AXES}
    core, zh, zl, yi = place["c"], place["zh"], place["zl"], place["yi"]
    own_arg = (yi * 16 + zl * 4 + core * 2)[None]
    at_arg = jnp.stack([zh, zl, core])
    home_arg = (place["x"] * 2 + place["yp"])[None]
    weight_t = jnp.swapaxes(up_weight, 1, 2)[0]
    hidden, width = weight_t.shape
    half = width // 2

    rows = placed_rows(tokens, routes.T)
    rows, weight_t = lax.optimization_barrier((rows, weight_t))
    arrived = lax.all_to_all(
        rows.reshape(16, 16, FOLD + EXTRA), FAR, split_axis=0, concat_axis=0, tiled=True
    ).reshape(256, FOLD + EXTRA)

    give = other_half(core[None], weight_t)
    other_t = swap(give, "c")
    ut, u = gated(jnp.swapaxes(gate_pre, 1, 2)[0], jnp.swapaxes(grad_hidden, 1, 2)[0])
    other_u = swap(u, "c")
    terms = terms_of(core[None], u, other_u, weight_t, other_t)
    back = lax.all_to_all(
        terms.reshape(16, 32, half), PLANE, split_axis=0, concat_axis=0, tiled=True
    ).reshape(512, half)

    two = unfold(home_arg, arrived, width)
    run = jnp.concatenate([two] + [cross(two, k) for k in (1, 2, 3)], axis=0)
    other_run = swap(run, "c")
    pair = swap(run, "yi")
    u_rows = ordered(own_arg, ut)
    choice = chooser(at_arg, run, other_run)

    sums = combined(choice, back)
    parts = lax.all_to_all(
        sums.reshape(8, PAD, half + half // 2), RING, split_axis=0, concat_axis=0, tiled=True
    )

    pair = lax.optimization_barrier((pair, sums))[0]
    rows = [run, pair, other_run, swap(pair, "c")]
    grad = weight_grad(u_rows, rows, width, 2048)

    mine, other = totalled(parts)
    other = swap(other, "c")
    left, right = jnp.where(core == 0, mine, other), jnp.where(core == 0, other, mine)
    grad_rows = jnp.concatenate([left, right], axis=1)[:TOK]
    return (grad_rows, jnp.swapaxes(grad[None], 1, 2))


def solution(mesh):
    fine = Mesh(mesh.devices.reshape(SIZES), AXES)
    part, column = AXES[:4], AXES[4:]
    in_specs = (
        P(AXES, None),
        P(AXES, None),
        P(part, None, column),
        P(part, None, column),
        P(part, None, column),
    )
    out_specs = (P(AXES, None), P(part, None, column))
    return jax.shard_map(body, mesh=fine, in_specs=in_specs, out_specs=out_specs, check_vma=False)
```

```python
import functools

import jax
import jax.numpy as jnp
from jax import lax
from jax.experimental import pallas as pl
from jax.experimental.pallas import tpu as pltpu
from jax.sharding import Mesh, PartitionSpec as P

EXPERTS = 16
CAP = 2
AXES = ("zh", "x", "yp", "yi", "zl", "c")
SIZES = (2, 4, 2, 2, 4, 2)
FAR = ("zh", "x", "yp")
PLANE = ("x", "yp", "yi")
RING = ("zh", "zl")
TOK = 6
PAD = 8
FOLD = 768
EXTRA = 128
MIB = 1 << 20
SMALL = pl.CostEstimate(flops=1000, bytes_accessed=1000, transcendentals=0)
BF, F32, I32 = jnp.bfloat16, jnp.float32, jnp.int32


def params(mib=24):
    return pltpu.CompilerParams(vmem_limit_bytes=mib * MIB)


def iota(shape, dim):
    return lax.broadcasted_iota(I32, shape, dim)


def gate_kernel(gate_ref, grad_ref, ut_ref, u_ref):
    gate = gate_ref[...].astype(F32)
    value = (grad_ref[...].astype(F32) * (gate / (1.0 + jnp.exp(-gate)))).astype(BF)
    ut_ref[...] = value
    u_ref[...] = value.T


def gated(gate_t, grad_t):
    hidden, rows = gate_t.shape
    return pl.pallas_call(
        gate_kernel,
        out_shape=(
            jax.ShapeDtypeStruct((hidden, rows), BF),
            jax.ShapeDtypeStruct((rows, hidden), BF),
        ),
        compiler_params=params(60),
        cost_estimate=pl.CostEstimate(flops=10**6, bytes_accessed=1400000, transcendentals=172032),
    )(gate_t, grad_t)


def copy_kernel(core_ref, in_ref, out_ref):
    out_ref[...] = in_ref[...]


def other_half(core, weight_t):
    hidden, width = weight_t.shape
    block = 1024
    steps = width // 2 // block
    return pl.pallas_call(
        copy_kernel,
        grid_spec=pltpu.PrefetchScalarGridSpec(
            num_scalar_prefetch=1,
            grid=(steps,),
            in_specs=[pl.BlockSpec((hidden, block), lambda i, core: (0, (1 - core[0]) * steps + i))],
            out_specs=pl.BlockSpec((hidden, block), lambda i, core: (0, i)),
        ),
        out_shape=jax.ShapeDtypeStruct((hidden, width // 2), BF),
        compiler_params=params(60),
        cost_estimate=pl.CostEstimate(flops=0, bytes_accessed=4200000, transcendentals=0),
    )(core, weight_t)


def terms_kernel(core_ref, u_ref, v_ref, w_ref, x_ref, out_ref):
    term = jnp.dot(u_ref[...], w_ref[...], preferred_element_type=F32)
    term += jnp.dot(v_ref[...], x_ref[...], preferred_element_type=F32)
    term = term.astype(BF).reshape(2, 16, 16, term.shape[1])
    out_ref[:, 0, :, :] = term[0]
    out_ref[:, 1, :, :] = term[1]


def terms_of(core, u, v, weight_t, other_t):
    rows, hidden = u.shape
    half = other_t.shape[1]
    block = 1024
    steps = half // block
    return pl.pallas_call(
        terms_kernel,
        grid_spec=pltpu.PrefetchScalarGridSpec(
            num_scalar_prefetch=1,
            grid=(steps,),
            in_specs=[
                pl.BlockSpec((rows, hidden), lambda i, core: (0, 0)),
                pl.BlockSpec((rows, hidden), lambda i, core: (0, 0)),
                pl.BlockSpec((hidden, block), lambda i, core: (0, core[0] * steps + i)),
                pl.BlockSpec((hidden, block), lambda i, core: (0, i)),
            ],
            out_specs=pl.BlockSpec((16, 2, 16, block), lambda i, core: (0, 0, 0, i)),
        ),
        out_shape=jax.ShapeDtypeStruct((16, 2, 16, half), BF),
        compiler_params=params(),
        cost_estimate=pl.CostEstimate(flops=4 * rows * hidden * half, bytes_accessed=8000000, transcendentals=0),
    )(core, u, v, weight_t, other_t)


def named_mask(routes, expert):
    named = jnp.zeros(expert.shape, F32)
    for k in range(4):
        named += jnp.where(routes[:, k : k + 1] == expert, 1.0, 0.0)
    return named


def place_kernel(tokens_ref, routes_ref, out_ref, held_ref, named_ref):
    count, width = tokens_ref.shape
    held_ref[...] = jnp.zeros(held_ref.shape, F32)
    held_ref[:count, :] = tokens_ref[...].astype(F32)
    named_ref[...] = jnp.full(named_ref.shape, -1.0, F32)
    named_ref[:count, :4] = routes_ref[...].astype(F32).T
    routes = named_ref[...]
    column = iota((PAD, 256), 1)
    named = named_mask(routes, (column // 16).astype(F32))
    lower = jnp.where(iota((PAD, PAD), 0) > iota((PAD, PAD), 1), 1.0, 0.0)
    before = jnp.dot(lower, named, preferred_element_type=F32)
    chosen = jnp.where(before == (column // 8 % 2).astype(F32), named, 0.0)
    folds = range(width // FOLD)
    pick = jnp.concatenate([jnp.where(column % 8 == fold, chosen, 0.0) for fold in folds], axis=0)
    pieces = [held_ref[:, fold * FOLD : fold * FOLD + FOLD] for fold in folds]
    pieces = jnp.concatenate(pieces, axis=0).astype(BF)
    total = jnp.dot(pick.T.astype(BF), pieces, preferred_element_type=F32)
    out_ref[:, :FOLD] = total.astype(BF)
    spread = jnp.where(iota((256, PAD), 0) % PAD == iota((256, PAD), 1), 1.0, 0.0).astype(BF)
    out_ref[:, FOLD:] = jnp.dot(spread, routes.astype(BF), preferred_element_type=F32).astype(BF)


def placed_rows(tokens, routes):
    return pl.pallas_call(
        place_kernel,
        out_shape=jax.ShapeDtypeStruct((256, FOLD + EXTRA), BF),
        scratch_shapes=[pltpu.VMEM((PAD, tokens.shape[1]), F32), pltpu.VMEM((PAD, EXTRA), F32)],
        compiler_params=params(60),
        cost_estimate=pl.CostEstimate(flops=10**6, bytes_accessed=500000, transcendentals=0),
    )(tokens, routes)


def routes_kernel(at_ref, rows_ref, out_ref):
    r, s = iota((16, 256), 0), iota((16, 256), 1)
    move = jnp.where(s == r // 8 * 128 + at_ref[0] * 16 + r % 8, 1.0, 0.0).astype(BF)
    out_ref[...] = jnp.dot(move, rows_ref[...], preferred_element_type=F32).astype(BF)


def own_routes(at, rows):
    return pl.pallas_call(
        routes_kernel,
        grid=(1,),
        in_specs=[
            pl.BlockSpec(memory_space=pltpu.SMEM),
            pl.BlockSpec((rows.shape[0], EXTRA), lambda i: (0, FOLD // EXTRA)),
        ],
        out_specs=pl.BlockSpec((16, EXTRA), lambda i: (0, 0)),
        out_shape=jax.ShapeDtypeStruct((16, EXTRA), BF),
        compiler_params=params(),
        cost_estimate=SMALL,
    )(at, rows)


def unfold_kernel(rows_ref, mine_ref, other_ref, out_ref):
    width = out_ref.shape[1] - EXTRA
    rows = rows_ref[...]
    r, s = iota((32, 256), 0), iota((32, 256), 1)
    for fold in range(width // FOLD):
        move = jnp.where(s == r * 8 + fold, 1.0, 0.0).astype(BF)
        piece = jnp.dot(move, rows[:, :FOLD], preferred_element_type=F32)
        out_ref[:, fold * FOLD : fold * FOLD + FOLD] = piece.astype(BF)
    out_ref[:, width:] = jnp.concatenate([mine_ref[...], other_ref[...]], axis=0)


def unfold(rows, mine, other, width):
    return pl.pallas_call(
        unfold_kernel,
        out_shape=jax.ShapeDtypeStruct((32, width + EXTRA), BF),
        compiler_params=params(),
        cost_estimate=pl.CostEstimate(flops=10**6, bytes_accessed=1000000, transcendentals=0),
    )(rows, mine, other)


def choose_kernel(at_ref, *refs):
    out_ref = refs[-1]
    shape = (8 * 2 * PAD, 512)
    row, column = iota(shape, 0), iota(shape, 1)
    expert = at_ref[0] * 8 + column // 64
    routes = jnp.concatenate([ref[...] for ref in refs[:-1]], axis=0)
    r, s = iota((128, 128), 0), iota((128, 128), 1)
    came = (4 - jnp.bitwise_xor((r // 16) % 4, at_ref[1])) % 4 * 32 + (r // 8) % 2 * 16 + r // 64 * 8 + r % 8
    move = jnp.where(came == s, 1.0, 0.0).astype(BF)
    named = named_mask(jnp.dot(move, routes, preferred_element_type=F32), expert.astype(F32))
    r, s = iota((128, 128), 0), iota((128, 128), 1)
    lower = jnp.where((r // PAD == s // PAD) & (r > s), 1.0, 0.0)
    before = jnp.dot(lower.astype(BF), named.astype(BF), preferred_element_type=F32)
    device = row // 16 * 2 + jnp.bitwise_xor((row // 8) % 2, at_ref[2])
    fits = (before == (column % 2).astype(F32)) & (device == (column // 2) % 16)
    chosen = jnp.where(fits, named, 0.0).astype(BF)
    r, s = iota((192, 128), 0), iota((192, 128), 1)
    late = r // 64
    token = r % 8 + jnp.where(late == 0, 0, 12 - 4 * late)
    real = (late == 0) | ((token >= 8) & (token < 12))
    place = r % 64 // 8 * 16 + token // TOK * PAD + token % TOK
    move = jnp.where((place == s) & real, 1.0, 0.0).astype(BF)
    out_ref[...] = jnp.dot(move, chosen, preferred_element_type=F32).astype(BF)


def chooser(at, *runs):
    last = runs[0].shape[1] // EXTRA - 1
    return pl.pallas_call(
        choose_kernel,
        grid=(1,),
        in_specs=[pl.BlockSpec(memory_space=pltpu.SMEM)]
        + [pl.BlockSpec((value.shape[0], EXTRA), lambda i: (0, last)) for value in runs],
        out_specs=pl.BlockSpec((192, 512), lambda i: (0, 0)),
        out_shape=jax.ShapeDtypeStruct((192, 512), BF),
        compiler_params=params(),
        cost_estimate=pl.CostEstimate(flops=10**6, bytes_accessed=200000, transcendentals=0),
    )(at, *runs)


def combine_kernel(choice_ref, back_ref, out_ref):
    half = back_ref.shape[1]
    step = half // 4
    for at in range(0, half // 2, step):
        low = jnp.dot(choice_ref[...], back_ref[:, at : at + step], preferred_element_type=F32)
        high = back_ref[:, half // 2 + at : half // 2 + at + step]
        high = jnp.dot(choice_ref[...], high, preferred_element_type=F32)
        out_ref[:, at : at + step] = low[:64].astype(BF)
        out_ref[:, half // 2 + at : half // 2 + at + step] = high[:64].astype(BF)
        out_ref[:, half + at : half + at + step] = (low[64:128] + high[128:]).astype(BF)


def combined(choice, back):
    rows, half = back.shape
    return pl.pallas_call(
        combine_kernel,
        out_shape=jax.ShapeDtypeStruct((64, half + half // 2), BF),
        compiler_params=params(),
        cost_estimate=pl.CostEstimate(flops=2 * 192 * rows * half, bytes_accessed=4000000, transcendentals=0),
    )(choice, back)


def total_kernel(parts_ref, mine_ref, other_ref):
    half = mine_ref.shape[1]
    total = parts_ref[0].astype(F32)
    for source in range(1, parts_ref.shape[0]):
        total += parts_ref[source].astype(F32)
    total = total.astype(BF)
    mine_ref[...] = total[:, :half]
    r, s = iota((PAD, PAD), 0), iota((PAD, PAD), 1)

    def moved(shift, keep, value):
        move = jnp.where((s == r + shift) & keep, 1.0, 0.0).astype(BF)
        return jnp.dot(move, value, preferred_element_type=F32)

    first = moved(TOK, r < 2, total[:, :half])
    second = (r >= 2) & (r < TOK)
    rest = total[:, half:]
    rest = jnp.concatenate([moved(-2, second, rest), moved(2, second, rest)], axis=1)
    other_ref[...] = (first + rest).astype(BF)


def totalled(parts):
    half = parts.shape[2] * 2 // 3
    like = jax.ShapeDtypeStruct((PAD, half), BF)
    return pl.pallas_call(
        total_kernel,
        out_shape=(like, like),
        compiler_params=params(),
        cost_estimate=SMALL,
    )(parts)


def order_kernel(own_ref, ut_ref, out_ref):
    row, column = iota((512, 512), 0), iota((512, 512), 1)
    near = (column // 128) % 2 * 16 + (4 - (column // 32) % 4) % 4 * 4 + column // 256 * 2
    origin = column % 32 // 2 * 32 + jnp.bitwise_xor(own_ref[0], near) + column % 2
    move = jnp.where(row == origin, 1.0, 0.0).astype(BF)
    out_ref[...] = jnp.dot(ut_ref[...], move, preferred_element_type=F32).astype(BF)


def ordered(own, ut):
    return pl.pallas_call(
        order_kernel,
        in_specs=[pl.BlockSpec(memory_space=pltpu.SMEM), pl.BlockSpec(memory_space=pltpu.VMEM)],
        out_shape=jax.ShapeDtypeStruct(ut.shape, BF),
        compiler_params=params(),
        cost_estimate=SMALL,
    )(own, ut)


def weight_kernel(count, u_ref, *refs):
    rows = jnp.concatenate([ref[...] for ref in refs[:count]], axis=0)
    refs[-1][...] = jnp.dot(u_ref[...], rows, preferred_element_type=F32).astype(BF)


def weight_grad(u, blocks, width, block):
    hidden = u.shape[0]
    specs = [pl.BlockSpec(u.shape, lambda i: (0, 0))]
    specs += [pl.BlockSpec((value.shape[0], block), lambda i: (0, i)) for value in blocks]
    return pl.pallas_call(
        functools.partial(weight_kernel, len(blocks)),
        grid=(width // block,),
        in_specs=specs,
        out_specs=pl.BlockSpec((hidden, block), lambda i: (0, i)),
        out_shape=jax.ShapeDtypeStruct((hidden, width), BF),
        compiler_params=params(),
        cost_estimate=pl.CostEstimate(
            flops=2 * hidden * 512 * width, bytes_accessed=2 * (512 + hidden) * width, transcendentals=0
        ),
    )(u, *blocks)


def swap(value, axis):
    return lax.ppermute(value, axis, [(0, 1), (1, 0)])


def cross(value, mask):
    return lax.ppermute(value, "zl", [(i, i ^ mask) for i in range(4)])


def body(tokens, routes, up_weight, gate_pre, grad_hidden):
    place = {name: lax.axis_index(name).astype(I32) for name in AXES}
    core, zh, zl, yi = place["c"], place["zh"], place["zl"], place["yi"]
    own_arg = (yi * 16 + zl * 4 + core * 2)[None]
    at_arg = jnp.stack([zh, zl, core])
    home_arg = (place["x"] * 2 + place["yp"])[None]
    weight_t = jnp.swapaxes(up_weight, 1, 2)[0]
    hidden, width = weight_t.shape
    half = width // 2

    rows = placed_rows(tokens, routes.T)
    rows, weight_t = lax.optimization_barrier((rows, weight_t))
    arrived = lax.all_to_all(
        rows.reshape(16, 16, FOLD + EXTRA), FAR, split_axis=0, concat_axis=0, tiled=True
    ).reshape(256, FOLD + EXTRA)

    give = other_half(core[None], weight_t)
    other_t = swap(give, "c")
    ut, u = gated(jnp.swapaxes(gate_pre, 1, 2)[0], jnp.swapaxes(grad_hidden, 1, 2)[0])
    other_u = swap(u, "c")
    terms = terms_of(core[None], u, other_u, weight_t, other_t)
    arrived, terms = lax.optimization_barrier((arrived, terms))
    back = lax.all_to_all(
        terms.reshape(16, 32, half), PLANE, split_axis=0, concat_axis=0, tiled=True
    ).reshape(512, half)

    near_routes = own_routes(home_arg, arrived)
    two = unfold(arrived, near_routes, swap(near_routes, "c"), width)
    near, far, far_too = (cross(two, k) for k in (3, 2, 1))
    early, late = jnp.concatenate([two, near], axis=0), jnp.concatenate([far, far_too], axis=0)
    early_pair = swap(early, "yi")
    other_early, other_late = swap(early, "c"), swap(late, "c")
    u_rows = ordered(own_arg, ut)
    choice = chooser(at_arg, early, late)

    sums = combined(choice, back)
    parts = lax.all_to_all(
        sums.reshape(8, PAD, half + half // 2), RING, split_axis=0, concat_axis=0, tiled=True
    )

    ready, _ = lax.optimization_barrier((late, sums))
    late_pair = swap(ready, "yi")
    other_early_pair = swap(early_pair, "c")
    parts, other_early, other_late, other_early_pair = lax.optimization_barrier(
        (parts, other_early, other_late, other_early_pair)
    )
    rows = [early, late, early_pair, late_pair, other_early, other_late]
    rows += [other_early_pair, swap(late_pair, "c")]
    grad = weight_grad(u_rows, rows, width, 2048)

    mine, other = totalled(parts)
    other = swap(other, "c")
    left, right = jnp.where(core == 0, mine, other), jnp.where(core == 0, other, mine)
    grad_rows = jnp.concatenate([left, right], axis=1)[:TOK]
    return (grad_rows, jnp.swapaxes(grad[None], 1, 2))


def solution(mesh):
    fine = Mesh(mesh.devices.reshape(SIZES), AXES)
    part, column = AXES[:4], AXES[4:]
    in_specs = (
        P(AXES, None),
        P(AXES, None),
        P(part, None, column),
        P(part, None, column),
        P(part, None, column),
    )
    out_specs = (P(AXES, None), P(part, None, column))
    return jax.shard_map(body, mesh=fine, in_specs=in_specs, out_specs=out_specs, check_vma=False)
```

```python
import functools

import jax
import jax.numpy as jnp
from jax import lax
from jax.experimental import pallas as pl
from jax.experimental.pallas import tpu as pltpu
from jax.sharding import Mesh, PartitionSpec as P

EXPERTS = 16
CAP = 2
AXES = ("zh", "x", "yp", "yi", "zl", "c")
SIZES = (2, 4, 2, 2, 4, 2)
FAR = ("x", "yp", "zh")
PLANE = ("x", "yp", "yi")
RING = ("zh", "zl")
TOK = 6
PAD = 8
FOLD = 768
EXTRA = 128
MIB = 1 << 20
SMALL = pl.CostEstimate(flops=1000, bytes_accessed=1000, transcendentals=0)
BF, F32, I32 = jnp.bfloat16, jnp.float32, jnp.int32


def params(mib=24):
    return pltpu.CompilerParams(vmem_limit_bytes=mib * MIB)


def iota(shape, dim):
    return lax.broadcasted_iota(I32, shape, dim)


def gate_kernel(gate_ref, grad_ref, ut_ref, u_ref):
    gate = gate_ref[...].astype(F32)
    value = (grad_ref[...].astype(F32) * (gate / (1.0 + jnp.exp(-gate)))).astype(BF)
    ut_ref[...] = value
    u_ref[...] = value.T


def gated(gate_t, grad_t):
    hidden, rows = gate_t.shape
    return pl.pallas_call(
        gate_kernel,
        out_shape=(
            jax.ShapeDtypeStruct((hidden, rows), BF),
            jax.ShapeDtypeStruct((rows, hidden), BF),
        ),
        compiler_params=params(60),
        cost_estimate=pl.CostEstimate(flops=10**6, bytes_accessed=1400000, transcendentals=172032),
    )(gate_t, grad_t)


def copy_kernel(core_ref, in_ref, out_ref):
    out_ref[...] = in_ref[...]


def other_half(core, weight_t):
    hidden, width = weight_t.shape
    block = 1024
    steps = width // 2 // block
    return pl.pallas_call(
        copy_kernel,
        grid_spec=pltpu.PrefetchScalarGridSpec(
            num_scalar_prefetch=1,
            grid=(steps,),
            in_specs=[pl.BlockSpec((hidden, block), lambda i, core: (0, (1 - core[0]) * steps + i))],
            out_specs=pl.BlockSpec((hidden, block), lambda i, core: (0, i)),
        ),
        out_shape=jax.ShapeDtypeStruct((hidden, width // 2), BF),
        compiler_params=params(60),
        cost_estimate=pl.CostEstimate(flops=0, bytes_accessed=4200000, transcendentals=0),
    )(core, weight_t)


def terms_kernel(core_ref, u_ref, v_ref, w_ref, x_ref, out_ref):
    term = jnp.dot(u_ref[...], w_ref[...], preferred_element_type=F32)
    term += jnp.dot(v_ref[...], x_ref[...], preferred_element_type=F32)
    term = term.astype(BF).reshape(2, 16, 16, term.shape[1])
    out_ref[:, 0, :, :] = term[0]
    out_ref[:, 1, :, :] = term[1]


def terms_of(core, u, v, weight_t, other_t):
    rows, hidden = u.shape
    half = other_t.shape[1]
    block = 1024
    steps = half // block
    return pl.pallas_call(
        terms_kernel,
        grid_spec=pltpu.PrefetchScalarGridSpec(
            num_scalar_prefetch=1,
            grid=(steps,),
            in_specs=[
                pl.BlockSpec((rows, hidden), lambda i, core: (0, 0)),
                pl.BlockSpec((rows, hidden), lambda i, core: (0, 0)),
                pl.BlockSpec((hidden, block), lambda i, core: (0, core[0] * steps + i)),
                pl.BlockSpec((hidden, block), lambda i, core: (0, i)),
            ],
            out_specs=pl.BlockSpec((16, 2, 16, block), lambda i, core: (0, 0, 0, i)),
        ),
        out_shape=jax.ShapeDtypeStruct((16, 2, 16, half), BF),
        compiler_params=params(),
        cost_estimate=pl.CostEstimate(flops=4 * rows * hidden * half, bytes_accessed=8000000, transcendentals=0),
    )(core, u, v, weight_t, other_t)


def named_mask(routes, expert):
    named = jnp.zeros(expert.shape, F32)
    for k in range(4):
        named += jnp.where(routes[:, k : k + 1] == expert, 1.0, 0.0)
    return named


def place_kernel(tokens_ref, routes_ref, out_ref, held_ref, named_ref):
    count, width = tokens_ref.shape
    held_ref[...] = jnp.zeros(held_ref.shape, F32)
    held_ref[:count, :] = tokens_ref[...].astype(F32)
    named_ref[...] = jnp.full(named_ref.shape, -1.0, F32)
    named_ref[:count, :4] = routes_ref[...].astype(F32).T
    routes = named_ref[...]
    column = iota((PAD, 256), 1)
    named = named_mask(routes, (column // 16 % 2 * 8 + column // 32).astype(F32))
    lower = jnp.where(iota((PAD, PAD), 0) > iota((PAD, PAD), 1), 1.0, 0.0)
    before = jnp.dot(lower, named, preferred_element_type=F32)
    chosen = jnp.where(before == (column // 8 % 2).astype(F32), named, 0.0)
    folds = range(width // FOLD)
    pick = jnp.concatenate([jnp.where(column % 8 == fold, chosen, 0.0) for fold in folds], axis=0)
    pieces = [held_ref[:, fold * FOLD : fold * FOLD + FOLD] for fold in folds]
    pieces = jnp.concatenate(pieces, axis=0).astype(BF)
    total = jnp.dot(pick.T.astype(BF), pieces, preferred_element_type=F32)
    out_ref[:, :FOLD] = total.astype(BF)
    spread = jnp.where(iota((256, PAD), 0) % PAD == iota((256, PAD), 1), 1.0, 0.0).astype(BF)
    out_ref[:, FOLD:] = jnp.dot(spread, routes.astype(BF), preferred_element_type=F32).astype(BF)


def placed_rows(tokens, routes):
    return pl.pallas_call(
        place_kernel,
        out_shape=jax.ShapeDtypeStruct((256, FOLD + EXTRA), BF),
        scratch_shapes=[pltpu.VMEM((PAD, tokens.shape[1]), F32), pltpu.VMEM((PAD, EXTRA), F32)],
        compiler_params=params(60),
        cost_estimate=pl.CostEstimate(flops=10**6, bytes_accessed=500000, transcendentals=0),
    )(tokens, routes)


def unfold_kernel(at_ref, rows_ref, out_ref):
    width = out_ref.shape[1] - EXTRA
    rows = rows_ref[...]
    r, s = iota((32, 256), 0), iota((32, 256), 1)
    for fold in range(width // FOLD):
        move = jnp.where(s == r * 8 + fold, 1.0, 0.0).astype(BF)
        piece = jnp.dot(move, rows[:, :FOLD], preferred_element_type=F32)
        out_ref[:, fold * FOLD : fold * FOLD + FOLD] = piece.astype(BF)
    move = jnp.where((s == (at_ref[0] * 2 + r // 8) * 16 + r % 8) & (r < 16), 1.0, 0.0).astype(BF)
    out_ref[:, width:] = jnp.dot(move, rows[:, FOLD:], preferred_element_type=F32).astype(BF)


def unfold(at, rows, width):
    return pl.pallas_call(
        unfold_kernel,
        in_specs=[pl.BlockSpec(memory_space=pltpu.SMEM), pl.BlockSpec(memory_space=pltpu.VMEM)],
        out_shape=jax.ShapeDtypeStruct((32, width + EXTRA), BF),
        compiler_params=params(),
        cost_estimate=pl.CostEstimate(flops=10**6, bytes_accessed=1000000, transcendentals=0),
    )(at, rows)


def choose_kernel(at_ref, *refs):
    out_ref = refs[-1]
    shape = (8 * 2 * PAD, 512)
    row, column = iota(shape, 0), iota(shape, 1)
    expert = at_ref[0] * 8 + column // 64
    routes = jnp.concatenate([ref[...] for ref in refs[:-1]], axis=0)
    r, s = iota((128, 256), 0), iota((128, 256), 1)
    came = (r // 8) % 2 * 128 + jnp.bitwise_xor((r // 16) % 4, at_ref[1]) * 32 + r // 64 * 8 + r % 8
    move = jnp.where(came == s, 1.0, 0.0).astype(BF)
    named = named_mask(jnp.dot(move, routes, preferred_element_type=F32), expert.astype(F32))
    r, s = iota((128, 128), 0), iota((128, 128), 1)
    lower = jnp.where((r // PAD == s // PAD) & (r > s), 1.0, 0.0)
    before = jnp.dot(lower.astype(BF), named.astype(BF), preferred_element_type=F32)
    device = row // 16 * 2 + jnp.bitwise_xor((row // 8) % 2, at_ref[2])
    fits = (before == (column % 2).astype(F32)) & (device == (column // 2) % 16)
    chosen = jnp.where(fits, named, 0.0).astype(BF)
    r, s = iota((192, 128), 0), iota((192, 128), 1)
    late = r // 64
    token = r % 8 + jnp.where(late == 0, 0, 12 - 4 * late)
    real = (late == 0) | ((token >= 8) & (token < 12))
    place = r % 64 // 8 * 16 + token // TOK * PAD + token % TOK
    move = jnp.where((place == s) & real, 1.0, 0.0).astype(BF)
    out_ref[...] = jnp.dot(move, chosen, preferred_element_type=F32).astype(BF)


def chooser(at, *runs):
    last = runs[0].shape[1] // EXTRA - 1
    return pl.pallas_call(
        choose_kernel,
        grid=(1,),
        in_specs=[pl.BlockSpec(memory_space=pltpu.SMEM)]
        + [pl.BlockSpec((value.shape[0], EXTRA), lambda i: (0, last)) for value in runs],
        out_specs=pl.BlockSpec((192, 512), lambda i: (0, 0)),
        out_shape=jax.ShapeDtypeStruct((192, 512), BF),
        compiler_params=params(),
        cost_estimate=pl.CostEstimate(flops=10**6, bytes_accessed=200000, transcendentals=0),
    )(at, *runs)


def combine_kernel(choice_ref, back_ref, out_ref):
    half = back_ref.shape[1]
    step = half // 4
    for at in range(0, half // 2, step):
        low = jnp.dot(choice_ref[...], back_ref[:, at : at + step], preferred_element_type=F32)
        high = back_ref[:, half // 2 + at : half // 2 + at + step]
        high = jnp.dot(choice_ref[...], high, preferred_element_type=F32)
        out_ref[:, at : at + step] = low[:64].astype(BF)
        out_ref[:, half // 2 + at : half // 2 + at + step] = high[:64].astype(BF)
        out_ref[:, half + at : half + at + step] = (low[64:128] + high[128:]).astype(BF)


def combined(choice, back):
    rows, half = back.shape
    return pl.pallas_call(
        combine_kernel,
        out_shape=jax.ShapeDtypeStruct((64, half + half // 2), BF),
        compiler_params=params(),
        cost_estimate=pl.CostEstimate(flops=2 * 192 * rows * half, bytes_accessed=4000000, transcendentals=0),
    )(choice, back)


def total_kernel(parts_ref, mine_ref, other_ref):
    half = mine_ref.shape[1]
    total = parts_ref[0].astype(F32)
    for source in range(1, parts_ref.shape[0]):
        total += parts_ref[source].astype(F32)
    total = total.astype(BF)
    mine_ref[...] = total[:, :half]
    r, s = iota((PAD, PAD), 0), iota((PAD, PAD), 1)

    def moved(shift, keep, value):
        move = jnp.where((s == r + shift) & keep, 1.0, 0.0).astype(BF)
        return jnp.dot(move, value, preferred_element_type=F32)

    first = moved(TOK, r < 2, total[:, :half])
    second = (r >= 2) & (r < TOK)
    rest = total[:, half:]
    rest = jnp.concatenate([moved(-2, second, rest), moved(2, second, rest)], axis=1)
    other_ref[...] = (first + rest).astype(BF)


def totalled(parts):
    half = parts.shape[2] * 2 // 3
    like = jax.ShapeDtypeStruct((PAD, half), BF)
    return pl.pallas_call(
        total_kernel,
        out_shape=(like, like),
        compiler_params=params(),
        cost_estimate=SMALL,
    )(parts)


def order_kernel(own_ref, ut_ref, out_ref):
    row, column = iota((512, 512), 0), iota((512, 512), 1)
    near = (column // 128) % 2 * 16 + (column // 32) % 4 * 4 + column // 256 * 2
    origin = column // 2 % 2 * 256 + column % 32 // 4 * 32 + jnp.bitwise_xor(own_ref[0], near) + column % 2
    move = jnp.where(row == origin, 1.0, 0.0).astype(BF)
    out_ref[...] = jnp.dot(ut_ref[...], move, preferred_element_type=F32).astype(BF)


def ordered(own, ut):
    return pl.pallas_call(
        order_kernel,
        in_specs=[pl.BlockSpec(memory_space=pltpu.SMEM), pl.BlockSpec(memory_space=pltpu.VMEM)],
        out_shape=jax.ShapeDtypeStruct(ut.shape, BF),
        compiler_params=params(),
        cost_estimate=SMALL,
    )(own, ut)


def weight_kernel(count, u_ref, *refs):
    rows = jnp.concatenate([ref[...] for ref in refs[:count]], axis=0)
    refs[-1][...] = jnp.dot(u_ref[...], rows, preferred_element_type=F32).astype(BF)


def weight_grad(u, blocks, width, block):
    hidden = u.shape[0]
    specs = [pl.BlockSpec(u.shape, lambda i: (0, 0))]
    specs += [pl.BlockSpec((value.shape[0], block), lambda i: (0, i)) for value in blocks]
    return pl.pallas_call(
        functools.partial(weight_kernel, len(blocks)),
        grid=(width // block,),
        in_specs=specs,
        out_specs=pl.BlockSpec((hidden, block), lambda i: (0, i)),
        out_shape=jax.ShapeDtypeStruct((hidden, width), BF),
        compiler_params=params(),
        cost_estimate=pl.CostEstimate(
            flops=2 * hidden * 512 * width, bytes_accessed=2 * (512 + hidden) * width, transcendentals=0
        ),
    )(u, *blocks)


def swap(value, axis):
    return lax.ppermute(value, axis, [(0, 1), (1, 0)])


def cross(value, mask):
    return lax.ppermute(value, "zl", [(i, i ^ mask) for i in range(4)])


def body(tokens, routes, up_weight, gate_pre, grad_hidden):
    place = {name: lax.axis_index(name).astype(I32) for name in AXES}
    core, zh, zl, yi = place["c"], place["zh"], place["zl"], place["yi"]
    own_arg = (yi * 16 + zl * 4 + core * 2)[None]
    at_arg = jnp.stack([zh, zl, core])
    home_arg = (place["x"] * 2 + place["yp"])[None]
    weight_t = jnp.swapaxes(up_weight, 1, 2)[0]
    hidden, width = weight_t.shape
    half = width // 2

    rows = placed_rows(tokens, routes.T)
    rows, weight_t = lax.optimization_barrier((rows, weight_t))
    arrived = lax.all_to_all(
        rows.reshape(16, 16, FOLD + EXTRA), FAR, split_axis=0, concat_axis=0, tiled=True
    ).reshape(256, FOLD + EXTRA)

    give = other_half(core[None], weight_t)
    other_t = swap(give, "c")
    ut, u = gated(jnp.swapaxes(gate_pre, 1, 2)[0], jnp.swapaxes(grad_hidden, 1, 2)[0])
    other_u = swap(u, "c")
    terms = terms_of(core[None], u, other_u, weight_t, other_t)
    back = lax.all_to_all(
        terms.reshape(16, 32, half), PLANE, split_axis=0, concat_axis=0, tiled=True
    ).reshape(512, half)

    two = unfold(home_arg, arrived, width)
    run = jnp.concatenate([two] + [cross(two, k) for k in (1, 2, 3)], axis=0)
    other_run = swap(run, "c")
    pair = swap(run, "yi")
    u_rows = ordered(own_arg, ut)
    choice = chooser(at_arg, run, other_run)

    sums = combined(choice, back)
    parts = lax.all_to_all(
        sums.reshape(8, PAD, half + half // 2), RING, split_axis=0, concat_axis=0, tiled=True
    )

    pair = lax.optimization_barrier((pair, sums))[0]
    rows = [run, pair, other_run, swap(pair, "c")]
    grad = weight_grad(u_rows, rows, width, 2048)

    mine, other = totalled(parts)
    other = swap(other, "c")
    left, right = jnp.where(core == 0, mine, other), jnp.where(core == 0, other, mine)
    grad_rows = jnp.concatenate([left, right], axis=1)[:TOK]
    return (grad_rows, jnp.swapaxes(grad[None], 1, 2))


def solution(mesh):
    fine = Mesh(mesh.devices.reshape(SIZES), AXES)
    part, column = AXES[:4], AXES[4:]
    in_specs = (
        P(AXES, None),
        P(AXES, None),
        P(part, None, column),
        P(part, None, column),
        P(part, None, column),
    )
    out_specs = (P(AXES, None), P(part, None, column))
    return jax.shard_map(body, mesh=fine, in_specs=in_specs, out_specs=out_specs, check_vma=False)
```

```python
import functools

import jax
import jax.numpy as jnp
from jax import lax
from jax.experimental import pallas as pl
from jax.experimental.pallas import tpu as pltpu
from jax.sharding import Mesh, PartitionSpec as P

EXPERTS = 16
CAP = 2
AXES = ("zh", "x", "yp", "yi", "zl", "c")
SIZES = (2, 4, 2, 2, 4, 2)
FAR = ("x", "yp", "zh")
PLANE = ("x", "yp", "yi")
RING = ("zh", "zl")
TOK = 6
PAD = 8
FOLD = 768
EXTRA = 128
MIB = 1 << 20
SMALL = pl.CostEstimate(flops=1000, bytes_accessed=1000, transcendentals=0)
BF, F32, I32 = jnp.bfloat16, jnp.float32, jnp.int32


def params(mib=24):
    return pltpu.CompilerParams(vmem_limit_bytes=mib * MIB)


def iota(shape, dim):
    return lax.broadcasted_iota(I32, shape, dim)


def gate_kernel(gate_ref, grad_ref, ut_ref, u_ref):
    gate = gate_ref[...].astype(F32)
    value = (grad_ref[...].astype(F32) * (gate / (1.0 + jnp.exp(-gate)))).astype(BF)
    ut_ref[...] = value
    u_ref[...] = value.T


def gated(gate_t, grad_t):
    hidden, rows = gate_t.shape
    return pl.pallas_call(
        gate_kernel,
        out_shape=(
            jax.ShapeDtypeStruct((hidden, rows), BF),
            jax.ShapeDtypeStruct((rows, hidden), BF),
        ),
        compiler_params=params(60),
        cost_estimate=pl.CostEstimate(flops=10**6, bytes_accessed=1400000, transcendentals=172032),
    )(gate_t, grad_t)


def terms_kernel(core_ref, u_ref, v_ref, w_ref, x_ref, out_ref):
    term = jnp.dot(u_ref[...], w_ref[...], preferred_element_type=F32)
    term += jnp.dot(v_ref[...], x_ref[...], preferred_element_type=F32)
    term = term.astype(BF).reshape(2, 16, 16, term.shape[1])
    out_ref[:, 0, :, :] = term[0]
    out_ref[:, 1, :, :] = term[1]


def terms_of(core, u, v, weight_t, other_t):
    rows, hidden = u.shape
    half = other_t.shape[1]
    block = 1024
    steps = half // block
    return pl.pallas_call(
        terms_kernel,
        grid_spec=pltpu.PrefetchScalarGridSpec(
            num_scalar_prefetch=1,
            grid=(steps,),
            in_specs=[
                pl.BlockSpec((rows, hidden), lambda i, core: (0, 0)),
                pl.BlockSpec((rows, hidden), lambda i, core: (0, 0)),
                pl.BlockSpec((hidden, block), lambda i, core: (0, core[0] * steps + i)),
                pl.BlockSpec((hidden, block), lambda i, core: (0, i)),
            ],
            out_specs=pl.BlockSpec((16, 2, 16, block), lambda i, core: (0, 0, 0, i)),
        ),
        out_shape=jax.ShapeDtypeStruct((16, 2, 16, half), BF),
        compiler_params=params(),
        cost_estimate=pl.CostEstimate(flops=4 * rows * hidden * half, bytes_accessed=8000000, transcendentals=0),
    )(core, u, v, weight_t, other_t)


def named_mask(routes, expert):
    named = jnp.zeros(expert.shape, F32)
    for k in range(4):
        named += jnp.where(routes[:, k : k + 1] == expert, 1.0, 0.0)
    return named


def front_kernel(core_ref, weight_ref, tokens_ref, routes_ref, give_ref, out_ref, held_ref, named_ref):
    give_ref[...] = weight_ref[...]

    @pl.when(pl.program_id(0) == 0)
    def place():
        place_kernel(tokens_ref, routes_ref, out_ref, held_ref, named_ref)


def place_kernel(tokens_ref, routes_ref, out_ref, held_ref, named_ref):
    count, width = tokens_ref.shape
    held_ref[...] = jnp.zeros(held_ref.shape, F32)
    held_ref[:count, :] = tokens_ref[...].astype(F32)
    named_ref[...] = jnp.full(named_ref.shape, -1.0, F32)
    named_ref[:count, :4] = routes_ref[...].astype(F32).T
    routes = named_ref[...]
    column = iota((PAD, 256), 1)
    named = named_mask(routes, (column // 16 % 2 * 8 + column // 32).astype(F32))
    lower = jnp.where(iota((PAD, PAD), 0) > iota((PAD, PAD), 1), 1.0, 0.0)
    before = jnp.dot(lower, named, preferred_element_type=F32)
    chosen = jnp.where(before == (column // 8 % 2).astype(F32), named, 0.0)
    folds = range(width // FOLD)
    pick = jnp.concatenate([jnp.where(column % 8 == fold, chosen, 0.0) for fold in folds], axis=0)
    pieces = [held_ref[:, fold * FOLD : fold * FOLD + FOLD] for fold in folds]
    pieces = jnp.concatenate(pieces, axis=0).astype(BF)
    total = jnp.dot(pick.T.astype(BF), pieces, preferred_element_type=F32)
    out_ref[:, :FOLD] = total.astype(BF)
    spread = jnp.where(iota((256, PAD), 0) % PAD == iota((256, PAD), 1), 1.0, 0.0).astype(BF)
    out_ref[:, FOLD:] = jnp.dot(spread, routes.astype(BF), preferred_element_type=F32).astype(BF)


def front(core, weight_t, tokens, routes):
    hidden, width = weight_t.shape
    block = 1024
    steps = width // 2 // block
    return pl.pallas_call(
        front_kernel,
        grid_spec=pltpu.PrefetchScalarGridSpec(
            num_scalar_prefetch=1,
            grid=(steps,),
            in_specs=[
                pl.BlockSpec((hidden, block), lambda i, core: (0, (1 - core[0]) * steps + i)),
                pl.BlockSpec(tokens.shape, lambda i, core: (0, 0)),
                pl.BlockSpec(routes.shape, lambda i, core: (0, 0)),
            ],
            out_specs=[
                pl.BlockSpec((hidden, block), lambda i, core: (0, i)),
                pl.BlockSpec((256, FOLD + EXTRA), lambda i, core: (0, 0)),
            ],
            scratch_shapes=[pltpu.VMEM((PAD, tokens.shape[1]), F32), pltpu.VMEM((PAD, EXTRA), F32)],
        ),
        out_shape=(
            jax.ShapeDtypeStruct((hidden, width // 2), BF),
            jax.ShapeDtypeStruct((256, FOLD + EXTRA), BF),
        ),
        compiler_params=params(60),
        cost_estimate=pl.CostEstimate(flops=10**6, bytes_accessed=4700000, transcendentals=0),
    )(core, weight_t, tokens, routes)


def unfold_kernel(at_ref, rows_ref, out_ref):
    width = out_ref.shape[1] - EXTRA
    rows = rows_ref[...]
    r, s = iota((32, 256), 0), iota((32, 256), 1)
    for fold in range(width // FOLD):
        move = jnp.where(s == r * 8 + fold, 1.0, 0.0).astype(BF)
        piece = jnp.dot(move, rows[:, :FOLD], preferred_element_type=F32)
        out_ref[:, fold * FOLD : fold * FOLD + FOLD] = piece.astype(BF)
    move = jnp.where((s == (at_ref[0] * 2 + r // 8) * 16 + r % 8) & (r < 16), 1.0, 0.0).astype(BF)
    out_ref[:, width:] = jnp.dot(move, rows[:, FOLD:], preferred_element_type=F32).astype(BF)


def unfold(at, rows, width):
    return pl.pallas_call(
        unfold_kernel,
        in_specs=[pl.BlockSpec(memory_space=pltpu.SMEM), pl.BlockSpec(memory_space=pltpu.VMEM)],
        out_shape=jax.ShapeDtypeStruct((32, width + EXTRA), BF),
        compiler_params=params(),
        cost_estimate=pl.CostEstimate(flops=10**6, bytes_accessed=1000000, transcendentals=0),
    )(at, rows)


def choose_kernel(at_ref, *refs):
    out_ref = refs[-1]
    shape = (8 * 2 * PAD, 512)
    row, column = iota(shape, 0), iota(shape, 1)
    expert = at_ref[0] * 8 + column // 64
    routes = jnp.concatenate([ref[...] for ref in refs[:-1]], axis=0)
    r, s = iota((128, 256), 0), iota((128, 256), 1)
    came = (r // 8) % 2 * 128 + jnp.bitwise_xor((r // 16) % 4, at_ref[1]) * 32 + r // 64 * 8 + r % 8
    move = jnp.where(came == s, 1.0, 0.0).astype(BF)
    named = named_mask(jnp.dot(move, routes, preferred_element_type=F32), expert.astype(F32))
    r, s = iota((128, 128), 0), iota((128, 128), 1)
    lower = jnp.where((r // PAD == s // PAD) & (r > s), 1.0, 0.0)
    before = jnp.dot(lower.astype(BF), named.astype(BF), preferred_element_type=F32)
    device = row // 16 * 2 + jnp.bitwise_xor((row // 8) % 2, at_ref[2])
    fits = (before == (column % 2).astype(F32)) & (device == (column // 2) % 16)
    chosen = jnp.where(fits, named, 0.0).astype(BF)
    r, s = iota((192, 128), 0), iota((192, 128), 1)
    late = r // 64
    token = r % 8 + jnp.where(late == 0, 0, 12 - 4 * late)
    real = (late == 0) | ((token >= 8) & (token < 12))
    place = r % 64 // 8 * 16 + token // TOK * PAD + token % TOK
    move = jnp.where((place == s) & real, 1.0, 0.0).astype(BF)
    out_ref[...] = jnp.dot(move, chosen, preferred_element_type=F32).astype(BF)


def chooser(at, *runs):
    last = runs[0].shape[1] // EXTRA - 1
    return pl.pallas_call(
        choose_kernel,
        grid=(1,),
        in_specs=[pl.BlockSpec(memory_space=pltpu.SMEM)]
        + [pl.BlockSpec((value.shape[0], EXTRA), lambda i: (0, last)) for value in runs],
        out_specs=pl.BlockSpec((192, 512), lambda i: (0, 0)),
        out_shape=jax.ShapeDtypeStruct((192, 512), BF),
        compiler_params=params(),
        cost_estimate=pl.CostEstimate(flops=10**6, bytes_accessed=200000, transcendentals=0),
    )(at, *runs)


def combine_kernel(choice_ref, back_ref, out_ref):
    half = back_ref.shape[1]
    step = half // 4
    for at in range(0, half // 2, step):
        low = jnp.dot(choice_ref[...], back_ref[:, at : at + step], preferred_element_type=F32)
        high = back_ref[:, half // 2 + at : half // 2 + at + step]
        high = jnp.dot(choice_ref[...], high, preferred_element_type=F32)
        out_ref[:, at : at + step] = low[:64].astype(BF)
        out_ref[:, half // 2 + at : half // 2 + at + step] = high[:64].astype(BF)
        out_ref[:, half + at : half + at + step] = (low[64:128] + high[128:]).astype(BF)


def combined(choice, back):
    rows, half = back.shape
    return pl.pallas_call(
        combine_kernel,
        out_shape=jax.ShapeDtypeStruct((64, half + half // 2), BF),
        compiler_params=params(),
        cost_estimate=pl.CostEstimate(flops=2 * 192 * rows * half, bytes_accessed=4000000, transcendentals=0),
    )(choice, back)


def total_kernel(parts_ref, mine_ref, other_ref):
    half = mine_ref.shape[1]
    total = parts_ref[0].astype(F32)
    for source in range(1, parts_ref.shape[0]):
        total += parts_ref[source].astype(F32)
    total = total.astype(BF)
    mine_ref[...] = total[:, :half]
    r, s = iota((PAD, PAD), 0), iota((PAD, PAD), 1)

    def moved(shift, keep, value):
        move = jnp.where((s == r + shift) & keep, 1.0, 0.0).astype(BF)
        return jnp.dot(move, value, preferred_element_type=F32)

    first = moved(TOK, r < 2, total[:, :half])
    second = (r >= 2) & (r < TOK)
    rest = total[:, half:]
    rest = jnp.concatenate([moved(-2, second, rest), moved(2, second, rest)], axis=1)
    other_ref[...] = (first + rest).astype(BF)


def totalled(parts):
    half = parts.shape[2] * 2 // 3
    like = jax.ShapeDtypeStruct((PAD, half), BF)
    return pl.pallas_call(
        total_kernel,
        out_shape=(like, like),
        compiler_params=params(),
        cost_estimate=SMALL,
    )(parts)


def order_kernel(own_ref, ut_ref, out_ref):
    row, column = iota((512, 512), 0), iota((512, 512), 1)
    near = (column // 128) % 2 * 16 + (column // 32) % 4 * 4 + column // 256 * 2
    origin = column // 2 % 2 * 256 + column % 32 // 4 * 32 + jnp.bitwise_xor(own_ref[0], near) + column % 2
    move = jnp.where(row == origin, 1.0, 0.0).astype(BF)
    out_ref[...] = jnp.dot(ut_ref[...], move, preferred_element_type=F32).astype(BF)


def ordered(own, ut):
    return pl.pallas_call(
        order_kernel,
        in_specs=[pl.BlockSpec(memory_space=pltpu.SMEM), pl.BlockSpec(memory_space=pltpu.VMEM)],
        out_shape=jax.ShapeDtypeStruct(ut.shape, BF),
        compiler_params=params(),
        cost_estimate=SMALL,
    )(own, ut)


def weight_kernel(count, u_ref, *refs):
    rows = jnp.concatenate([ref[...] for ref in refs[:count]], axis=0)
    refs[-1][...] = jnp.dot(u_ref[...], rows, preferred_element_type=F32).astype(BF)


def weight_grad(u, blocks, width, block):
    hidden = u.shape[0]
    specs = [pl.BlockSpec(u.shape, lambda i: (0, 0))]
    specs += [pl.BlockSpec((value.shape[0], block), lambda i: (0, i)) for value in blocks]
    return pl.pallas_call(
        functools.partial(weight_kernel, len(blocks)),
        grid=(width // block,),
        in_specs=specs,
        out_specs=pl.BlockSpec((hidden, block), lambda i: (0, i)),
        out_shape=jax.ShapeDtypeStruct((hidden, width), BF),
        compiler_params=params(),
        cost_estimate=pl.CostEstimate(
            flops=2 * hidden * 512 * width, bytes_accessed=2 * (512 + hidden) * width, transcendentals=0
        ),
    )(u, *blocks)


def swap(value, axis):
    return lax.ppermute(value, axis, [(0, 1), (1, 0)])


def cross(value, mask):
    return lax.ppermute(value, "zl", [(i, i ^ mask) for i in range(4)])


def body(tokens, routes, up_weight, gate_pre, grad_hidden):
    place = {name: lax.axis_index(name).astype(I32) for name in AXES}
    core, zh, zl, yi = place["c"], place["zh"], place["zl"], place["yi"]
    own_arg = (yi * 16 + zl * 4 + core * 2)[None]
    at_arg = jnp.stack([zh, zl, core])
    home_arg = (place["x"] * 2 + place["yp"])[None]
    weight_t = jnp.swapaxes(up_weight, 1, 2)[0]
    hidden, width = weight_t.shape
    half = width // 2

    give, rows = front(core[None], weight_t, tokens, routes.T)
    arrived = lax.all_to_all(
        rows.reshape(16, 16, FOLD + EXTRA), FAR, split_axis=0, concat_axis=0, tiled=True
    ).reshape(256, FOLD + EXTRA)

    other_t = swap(give, "c")
    ut, u = gated(jnp.swapaxes(gate_pre, 1, 2)[0], jnp.swapaxes(grad_hidden, 1, 2)[0])
    other_u = swap(u, "c")
    terms = terms_of(core[None], u, other_u, weight_t, other_t)
    back = lax.all_to_all(
        terms.reshape(16, 32, half), PLANE, split_axis=0, concat_axis=0, tiled=True
    ).reshape(512, half)

    two = unfold(home_arg, arrived, width)
    run = jnp.concatenate([two] + [cross(two, k) for k in (1, 2, 3)], axis=0)
    other_run = swap(run, "c")
    pair = swap(run, "yi")
    u_rows = ordered(own_arg, ut)
    choice = chooser(at_arg, run, other_run)

    sums = combined(choice, back)
    parts = lax.all_to_all(
        sums.reshape(8, PAD, half + half // 2), RING, split_axis=0, concat_axis=0, tiled=True
    )

    pair = lax.optimization_barrier((pair, sums))[0]
    rows = [run, pair, other_run, swap(pair, "c")]
    grad = weight_grad(u_rows, rows, width, 2048)

    mine, other = totalled(parts)
    other = swap(other, "c")
    left, right = jnp.where(core == 0, mine, other), jnp.where(core == 0, other, mine)
    grad_rows = jnp.concatenate([left, right], axis=1)[:TOK]
    return (grad_rows, jnp.swapaxes(grad[None], 1, 2))


def solution(mesh):
    fine = Mesh(mesh.devices.reshape(SIZES), AXES)
    part, column = AXES[:4], AXES[4:]
    in_specs = (
        P(AXES, None),
        P(AXES, None),
        P(part, None, column),
        P(part, None, column),
        P(part, None, column),
    )
    out_specs = (P(AXES, None), P(part, None, column))
    return jax.shard_map(body, mesh=fine, in_specs=in_specs, out_specs=out_specs, check_vma=False)
```

```python
import functools

import jax
import jax.numpy as jnp
from jax import lax
from jax.experimental import pallas as pl
from jax.experimental.pallas import tpu as pltpu
from jax.sharding import Mesh, PartitionSpec as P

EXPERTS = 16
CAP = 2
AXES = ("zh", "x", "yp", "yi", "zl", "c")
SIZES = (2, 4, 2, 2, 4, 2)
FAR = ("x", "yp", "zh")
PLANE = ("x", "yp", "yi")
RING = ("zh", "zl")
TOK = 6
PAD = 8
FOLD = 768
EXTRA = 128
MIB = 1 << 20
SMALL = pl.CostEstimate(flops=1000, bytes_accessed=1000, transcendentals=0)
BF, F32, I32 = jnp.bfloat16, jnp.float32, jnp.int32


def params(mib=24):
    return pltpu.CompilerParams(vmem_limit_bytes=mib * MIB)


def iota(shape, dim):
    return lax.broadcasted_iota(I32, shape, dim)


def gate_kernel(gate_ref, grad_ref, ut_ref, u_ref):
    gate = gate_ref[...].astype(F32)
    value = (grad_ref[...].astype(F32) * (gate / (1.0 + jnp.exp(-gate)))).astype(BF)
    ut_ref[...] = value
    u_ref[...] = value.T


def gated(gate_t, grad_t):
    hidden, rows = gate_t.shape
    return pl.pallas_call(
        gate_kernel,
        out_shape=(
            jax.ShapeDtypeStruct((hidden, rows), BF),
            jax.ShapeDtypeStruct((rows, hidden), BF),
        ),
        compiler_params=params(60),
        cost_estimate=pl.CostEstimate(flops=10**6, bytes_accessed=1400000, transcendentals=172032),
    )(gate_t, grad_t)


def terms_kernel(core_ref, u_ref, v_ref, w_ref, x_ref, out_ref):
    term = jnp.dot(u_ref[...], w_ref[...], preferred_element_type=F32)
    term += jnp.dot(v_ref[...], x_ref[...], preferred_element_type=F32)
    term = term.astype(BF).reshape(2, 16, 16, term.shape[1])
    out_ref[:, 0, :, :] = term[0]
    out_ref[:, 1, :, :] = term[1]


def terms_of(core, u, v, weight_t, other_t):
    rows, hidden = u.shape
    half = other_t.shape[1]
    block = 1024
    steps = half // block
    return pl.pallas_call(
        terms_kernel,
        grid_spec=pltpu.PrefetchScalarGridSpec(
            num_scalar_prefetch=1,
            grid=(steps,),
            in_specs=[
                pl.BlockSpec((rows, hidden), lambda i, core: (0, 0)),
                pl.BlockSpec((rows, hidden), lambda i, core: (0, 0)),
                pl.BlockSpec((hidden, block), lambda i, core: (0, core[0] * steps + i)),
                pl.BlockSpec((hidden, block), lambda i, core: (0, i)),
            ],
            out_specs=pl.BlockSpec((16, 2, 16, block), lambda i, core: (0, 0, 0, i)),
        ),
        out_shape=jax.ShapeDtypeStruct((16, 2, 16, half), BF),
        compiler_params=params(),
        cost_estimate=pl.CostEstimate(flops=4 * rows * hidden * half, bytes_accessed=8000000, transcendentals=0),
    )(core, u, v, weight_t, other_t)


def named_mask(routes, expert):
    named = jnp.zeros(expert.shape, F32)
    for k in range(4):
        named += jnp.where(routes[:, k : k + 1] == expert, 1.0, 0.0)
    return named


def front_kernel(core_ref, weight_ref, tokens_ref, routes_ref, give_ref, out_ref, held_ref, named_ref):
    give_ref[...] = weight_ref[...]

    @pl.when(pl.program_id(0) == 0)
    def place():
        place_kernel(tokens_ref, routes_ref, out_ref, held_ref, named_ref)


def place_kernel(tokens_ref, routes_ref, out_ref, held_ref, named_ref):
    count, width = tokens_ref.shape
    held_ref[...] = jnp.zeros(held_ref.shape, F32)
    held_ref[:count, :] = tokens_ref[...].astype(F32)
    named_ref[...] = jnp.full(named_ref.shape, -1.0, F32)
    named_ref[:count, :4] = routes_ref[...].astype(F32).T
    routes = named_ref[...]
    column = iota((PAD, 256), 1)
    named = named_mask(routes, (column // 16 % 2 * 8 + column // 32).astype(F32))
    lower = jnp.where(iota((PAD, PAD), 0) > iota((PAD, PAD), 1), 1.0, 0.0)
    before = jnp.dot(lower, named, preferred_element_type=F32)
    chosen = jnp.where(before == (column // 8 % 2).astype(F32), named, 0.0)
    folds = range(width // FOLD)
    pick = jnp.concatenate([jnp.where(column % 8 == fold, chosen, 0.0) for fold in folds], axis=0)
    pieces = [held_ref[:, fold * FOLD : fold * FOLD + FOLD] for fold in folds]
    pieces = jnp.concatenate(pieces, axis=0).astype(BF)
    total = jnp.dot(pick.T.astype(BF), pieces, preferred_element_type=F32)
    out_ref[:, :FOLD] = total.astype(BF)
    spread = jnp.where(iota((256, PAD), 0) % PAD == iota((256, PAD), 1), 1.0, 0.0).astype(BF)
    out_ref[:, FOLD:] = jnp.dot(spread, routes.astype(BF), preferred_element_type=F32).astype(BF)


def front(core, weight_t, tokens, routes):
    hidden, width = weight_t.shape
    block = 1024
    steps = width // 2 // block
    return pl.pallas_call(
        front_kernel,
        grid_spec=pltpu.PrefetchScalarGridSpec(
            num_scalar_prefetch=1,
            grid=(steps,),
            in_specs=[
                pl.BlockSpec((hidden, block), lambda i, core: (0, (1 - core[0]) * steps + i)),
                pl.BlockSpec(tokens.shape, lambda i, core: (0, 0)),
                pl.BlockSpec(routes.shape, lambda i, core: (0, 0)),
            ],
            out_specs=[
                pl.BlockSpec((hidden, block), lambda i, core: (0, i)),
                pl.BlockSpec((256, FOLD + EXTRA), lambda i, core: (0, 0)),
            ],
            scratch_shapes=[pltpu.VMEM((PAD, tokens.shape[1]), F32), pltpu.VMEM((PAD, EXTRA), F32)],
        ),
        out_shape=(
            jax.ShapeDtypeStruct((hidden, width // 2), BF),
            jax.ShapeDtypeStruct((256, FOLD + EXTRA), BF),
        ),
        compiler_params=params(60),
        cost_estimate=pl.CostEstimate(flops=10**6, bytes_accessed=4700000, transcendentals=0),
    )(core, weight_t, tokens, routes)


def unfold_kernel(at_ref, rows_ref, out_ref):
    width = out_ref.shape[1] - EXTRA
    rows = rows_ref[...]
    r, s = iota((32, 256), 0), iota((32, 256), 1)
    for fold in range(width // FOLD):
        move = jnp.where(s == r * 8 + fold, 1.0, 0.0).astype(BF)
        piece = jnp.dot(move, rows[:, :FOLD], preferred_element_type=F32)
        out_ref[:, fold * FOLD : fold * FOLD + FOLD] = piece.astype(BF)
    move = jnp.where((s == (at_ref[0] * 2 + r // 8) * 16 + r % 8) & (r < 16), 1.0, 0.0).astype(BF)
    out_ref[:, width:] = jnp.dot(move, rows[:, FOLD:], preferred_element_type=F32).astype(BF)


def unfold(at, rows, width):
    return pl.pallas_call(
        unfold_kernel,
        in_specs=[pl.BlockSpec(memory_space=pltpu.SMEM), pl.BlockSpec(memory_space=pltpu.VMEM)],
        out_shape=jax.ShapeDtypeStruct((32, width + EXTRA), BF),
        compiler_params=params(),
        cost_estimate=pl.CostEstimate(flops=10**6, bytes_accessed=1000000, transcendentals=0),
    )(at, rows)


def choose_kernel(at_ref, *refs):
    out_ref = refs[-1]
    shape = (8 * 2 * PAD, 512)
    row, column = iota(shape, 0), iota(shape, 1)
    expert = at_ref[0] * 8 + column // 64
    routes = jnp.concatenate([ref[...] for ref in refs[:-1]], axis=0)
    r, s = iota((128, 256), 0), iota((128, 256), 1)
    came = (r // 8) % 2 * 128 + jnp.bitwise_xor((r // 16) % 4, at_ref[1]) * 32 + r // 64 * 8 + r % 8
    move = jnp.where(came == s, 1.0, 0.0).astype(BF)
    named = named_mask(jnp.dot(move, routes, preferred_element_type=F32), expert.astype(F32))
    r, s = iota((128, 128), 0), iota((128, 128), 1)
    lower = jnp.where((r // PAD == s // PAD) & (r > s), 1.0, 0.0)
    before = jnp.dot(lower.astype(BF), named.astype(BF), preferred_element_type=F32)
    device = row // 16 * 2 + jnp.bitwise_xor((row // 8) % 2, at_ref[2])
    fits = (before == (column % 2).astype(F32)) & (device == (column // 2) % 16)
    chosen = jnp.where(fits, named, 0.0).astype(BF)
    r, s = iota((192, 128), 0), iota((192, 128), 1)
    late = r // 64
    token = r % 8 + jnp.where(late == 0, 0, 12 - 4 * late)
    real = (late == 0) | ((token >= 8) & (token < 12))
    place = r % 64 // 8 * 16 + token // TOK * PAD + token % TOK
    move = jnp.where((place == s) & real, 1.0, 0.0).astype(BF)
    out_ref[...] = jnp.dot(move, chosen, preferred_element_type=F32).astype(BF)


def chooser(at, *runs):
    last = runs[0].shape[1] // EXTRA - 1
    return pl.pallas_call(
        choose_kernel,
        grid=(1,),
        in_specs=[pl.BlockSpec(memory_space=pltpu.SMEM)]
        + [pl.BlockSpec((value.shape[0], EXTRA), lambda i: (0, last)) for value in runs],
        out_specs=pl.BlockSpec((192, 512), lambda i: (0, 0)),
        out_shape=jax.ShapeDtypeStruct((192, 512), BF),
        compiler_params=params(),
        cost_estimate=pl.CostEstimate(flops=10**6, bytes_accessed=200000, transcendentals=0),
    )(at, *runs)


def combine_kernel(choice_ref, back_ref, out_ref):
    half = back_ref.shape[1]
    step = half // 4
    for at in range(0, half // 2, step):
        low = jnp.dot(choice_ref[...], back_ref[:, at : at + step], preferred_element_type=F32)
        high = back_ref[:, half // 2 + at : half // 2 + at + step]
        high = jnp.dot(choice_ref[...], high, preferred_element_type=F32)
        out_ref[:, at : at + step] = low[:64].astype(BF)
        out_ref[:, half // 2 + at : half // 2 + at + step] = high[:64].astype(BF)
        out_ref[:, half + at : half + at + step] = (low[64:128] + high[128:]).astype(BF)


def combined(choice, back):
    rows, half = back.shape
    return pl.pallas_call(
        combine_kernel,
        out_shape=jax.ShapeDtypeStruct((64, half + half // 2), BF),
        compiler_params=params(),
        cost_estimate=pl.CostEstimate(flops=2 * 192 * rows * half, bytes_accessed=4000000, transcendentals=0),
    )(choice, back)


def total_kernel(parts_ref, mine_ref, other_ref):
    half = mine_ref.shape[1]
    total = parts_ref[0].astype(F32)
    for source in range(1, parts_ref.shape[0]):
        total += parts_ref[source].astype(F32)
    total = total.astype(BF)
    mine_ref[...] = total[:, :half]
    r, s = iota((PAD, PAD), 0), iota((PAD, PAD), 1)

    def moved(shift, keep, value):
        move = jnp.where((s == r + shift) & keep, 1.0, 0.0).astype(BF)
        return jnp.dot(move, value, preferred_element_type=F32)

    first = moved(TOK, r < 2, total[:, :half])
    second = (r >= 2) & (r < TOK)
    rest = total[:, half:]
    rest = jnp.concatenate([moved(-2, second, rest), moved(2, second, rest)], axis=1)
    other_ref[...] = (first + rest).astype(BF)


def totalled(parts):
    half = parts.shape[2] * 2 // 3
    like = jax.ShapeDtypeStruct((PAD, half), BF)
    return pl.pallas_call(
        total_kernel,
        out_shape=(like, like),
        compiler_params=params(),
        cost_estimate=SMALL,
    )(parts)


def order_kernel(own_ref, ut_ref, out_ref):
    row, column = iota((512, 512), 0), iota((512, 512), 1)
    near = (column // 128) % 2 * 16 + (column // 32) % 4 * 4 + column // 256 * 2
    origin = column // 2 % 2 * 256 + column % 32 // 4 * 32 + jnp.bitwise_xor(own_ref[0], near) + column % 2
    move = jnp.where(row == origin, 1.0, 0.0).astype(BF)
    out_ref[...] = jnp.dot(ut_ref[...], move, preferred_element_type=F32).astype(BF)


def ordered(own, ut):
    return pl.pallas_call(
        order_kernel,
        in_specs=[pl.BlockSpec(memory_space=pltpu.SMEM), pl.BlockSpec(memory_space=pltpu.VMEM)],
        out_shape=jax.ShapeDtypeStruct(ut.shape, BF),
        compiler_params=params(),
        cost_estimate=SMALL,
    )(own, ut)


def weight_kernel(count, u_ref, *refs):
    rows = jnp.concatenate([ref[...] for ref in refs[:count]], axis=0)
    refs[-1][...] = jnp.dot(u_ref[...], rows, preferred_element_type=F32).astype(BF)


def weight_grad(u, blocks, width, block):
    hidden = u.shape[0]
    specs = [pl.BlockSpec(u.shape, lambda i: (0, 0))]
    specs += [pl.BlockSpec((value.shape[0], block), lambda i: (0, i)) for value in blocks]
    return pl.pallas_call(
        functools.partial(weight_kernel, len(blocks)),
        grid=(width // block,),
        in_specs=specs,
        out_specs=pl.BlockSpec((hidden, block), lambda i: (0, i)),
        out_shape=jax.ShapeDtypeStruct((hidden, width), BF),
        compiler_params=params(),
        cost_estimate=pl.CostEstimate(
            flops=2 * hidden * 512 * width, bytes_accessed=2 * (512 + hidden) * width, transcendentals=0
        ),
    )(u, *blocks)


def swap(value, axis):
    return lax.ppermute(value, axis, [(0, 1), (1, 0)])


def cross(value, mask):
    return lax.ppermute(value, "zl", [(i, i ^ mask) for i in range(4)])


def body(tokens, routes, up_weight, gate_pre, grad_hidden):
    place = {name: lax.axis_index(name).astype(I32) for name in AXES}
    core, zh, zl, yi = place["c"], place["zh"], place["zl"], place["yi"]
    own_arg = (yi * 16 + zl * 4 + core * 2)[None]
    at_arg = jnp.stack([zh, zl, core])
    home_arg = (place["x"] * 2 + place["yp"])[None]
    weight_t = jnp.swapaxes(up_weight, 1, 2)[0]
    hidden, width = weight_t.shape
    half = width // 2

    give, rows = front(core[None], weight_t, tokens, routes.T)
    arrived = lax.all_to_all(
        rows.reshape(16, 16, FOLD + EXTRA), FAR, split_axis=0, concat_axis=0, tiled=True
    ).reshape(256, FOLD + EXTRA)

    other_t = swap(give, "c")
    ut, u = gated(jnp.swapaxes(gate_pre, 1, 2)[0], jnp.swapaxes(grad_hidden, 1, 2)[0])
    other_u = swap(u, "c")
    terms = terms_of(core[None], u, other_u, weight_t, other_t)
    back = lax.all_to_all(
        terms.reshape(16, 32, half), PLANE, split_axis=0, concat_axis=0, tiled=True
    ).reshape(512, half)

    two = unfold(home_arg, arrived, width)
    run = jnp.concatenate([two] + [cross(two, k) for k in (1, 2, 3)], axis=0)
    other_run = swap(run, "c")
    pair = swap(run, "yi")
    u_rows = ordered(own_arg, ut)
    choice = chooser(at_arg, run, other_run)

    sums = combined(choice, back)
    parts = lax.all_to_all(
        sums.reshape(8, PAD, half + half // 2), RING, split_axis=0, concat_axis=0, tiled=True
    )

    mine, other = totalled(parts)
    other = swap(other, "c")

    pair = lax.optimization_barrier((pair, sums))[0]
    pair, other = lax.optimization_barrier((pair, other))
    rows = [run, pair, other_run, swap(pair, "c")]
    grad = weight_grad(u_rows, rows, width, 2048)

    left, right = jnp.where(core == 0, mine, other), jnp.where(core == 0, other, mine)
    grad_rows = jnp.concatenate([left, right], axis=1)[:TOK]
    return (grad_rows, jnp.swapaxes(grad[None], 1, 2))


def solution(mesh):
    fine = Mesh(mesh.devices.reshape(SIZES), AXES)
    part, column = AXES[:4], AXES[4:]
    in_specs = (
        P(AXES, None),
        P(AXES, None),
        P(part, None, column),
        P(part, None, column),
        P(part, None, column),
    )
    out_specs = (P(AXES, None), P(part, None, column))
    return jax.shard_map(body, mesh=fine, in_specs=in_specs, out_specs=out_specs, check_vma=False)
```

```python
import functools

import jax
import jax.numpy as jnp
from jax import lax
from jax.experimental import pallas as pl
from jax.experimental.pallas import tpu as pltpu
from jax.sharding import Mesh, PartitionSpec as P

EXPERTS = 16
CAP = 2
AXES = ("zh", "x", "yp", "yi", "zl", "c")
SIZES = (2, 4, 2, 2, 4, 2)
FAR = ("x", "yp", "zh")
PLANE = ("yp", "yi", "x")
RING = ("zh", "zl")
TOK = 6
PAD = 8
FOLD = 768
EXTRA = 128
MIB = 1 << 20
SMALL = pl.CostEstimate(flops=1000, bytes_accessed=1000, transcendentals=0)
BF, F32, I32 = jnp.bfloat16, jnp.float32, jnp.int32


def params(mib=24):
    return pltpu.CompilerParams(vmem_limit_bytes=mib * MIB)


def iota(shape, dim):
    return lax.broadcasted_iota(I32, shape, dim)


def gate_kernel(gate_ref, grad_ref, ut_ref, u_ref):
    gate = gate_ref[...].astype(F32)
    value = (grad_ref[...].astype(F32) * (gate / (1.0 + jnp.exp(-gate)))).astype(BF)
    ut_ref[...] = value
    u_ref[...] = value.T


def gated(gate_t, grad_t):
    hidden, rows = gate_t.shape
    return pl.pallas_call(
        gate_kernel,
        out_shape=(
            jax.ShapeDtypeStruct((hidden, rows), BF),
            jax.ShapeDtypeStruct((rows, hidden), BF),
        ),
        compiler_params=params(60),
        cost_estimate=pl.CostEstimate(flops=10**6, bytes_accessed=1400000, transcendentals=172032),
    )(gate_t, grad_t)


def terms_kernel(core_ref, u_ref, v_ref, w_ref, x_ref, out_ref):
    term = jnp.dot(u_ref[...], w_ref[...], preferred_element_type=F32)
    term += jnp.dot(v_ref[...], x_ref[...], preferred_element_type=F32)
    term = term.astype(BF).reshape(2, 16, 16, term.shape[1])
    for zh in range(2):
        for place in range(16):
            out_ref[place % 4 * 4 + place // 4, zh, :, :] = term[zh, place]


def terms_of(core, u, v, weight_t, other_t):
    rows, hidden = u.shape
    half = other_t.shape[1]
    block = 1024
    steps = half // block
    return pl.pallas_call(
        terms_kernel,
        grid_spec=pltpu.PrefetchScalarGridSpec(
            num_scalar_prefetch=1,
            grid=(steps,),
            in_specs=[
                pl.BlockSpec((rows, hidden), lambda i, core: (0, 0)),
                pl.BlockSpec((rows, hidden), lambda i, core: (0, 0)),
                pl.BlockSpec((hidden, block), lambda i, core: (0, core[0] * steps + i)),
                pl.BlockSpec((hidden, block), lambda i, core: (0, i)),
            ],
            out_specs=pl.BlockSpec((16, 2, 16, block), lambda i, core: (0, 0, 0, i)),
        ),
        out_shape=jax.ShapeDtypeStruct((16, 2, 16, half), BF),
        compiler_params=params(),
        cost_estimate=pl.CostEstimate(flops=4 * rows * hidden * half, bytes_accessed=8000000, transcendentals=0),
    )(core, u, v, weight_t, other_t)


def named_mask(routes, expert):
    named = jnp.zeros(expert.shape, F32)
    for k in range(4):
        named += jnp.where(routes[:, k : k + 1] == expert, 1.0, 0.0)
    return named


def front_kernel(core_ref, weight_ref, tokens_ref, routes_ref, give_ref, out_ref, held_ref, named_ref):
    give_ref[...] = weight_ref[...]

    @pl.when(pl.program_id(0) == 0)
    def place():
        place_kernel(tokens_ref, routes_ref, out_ref, held_ref, named_ref)


def place_kernel(tokens_ref, routes_ref, out_ref, held_ref, named_ref):
    count, width = tokens_ref.shape
    held_ref[...] = jnp.zeros(held_ref.shape, F32)
    held_ref[:count, :] = tokens_ref[...].astype(F32)
    named_ref[...] = jnp.full(named_ref.shape, -1.0, F32)
    named_ref[:count, :4] = routes_ref[...].astype(F32).T
    routes = named_ref[...]
    column = iota((PAD, 256), 1)
    named = named_mask(routes, (column // 16 % 2 * 8 + column // 32).astype(F32))
    lower = jnp.where(iota((PAD, PAD), 0) > iota((PAD, PAD), 1), 1.0, 0.0)
    before = jnp.dot(lower, named, preferred_element_type=F32)
    chosen = jnp.where(before == (column // 8 % 2).astype(F32), named, 0.0)
    folds = range(width // FOLD)
    pick = jnp.concatenate([jnp.where(column % 8 == fold, chosen, 0.0) for fold in folds], axis=0)
    pieces = [held_ref[:, fold * FOLD : fold * FOLD + FOLD] for fold in folds]
    pieces = jnp.concatenate(pieces, axis=0).astype(BF)
    total = jnp.dot(pick.T.astype(BF), pieces, preferred_element_type=F32)
    out_ref[:, :FOLD] = total.astype(BF)
    spread = jnp.where(iota((256, PAD), 0) % PAD == iota((256, PAD), 1), 1.0, 0.0).astype(BF)
    out_ref[:, FOLD:] = jnp.dot(spread, routes.astype(BF), preferred_element_type=F32).astype(BF)


def front(core, weight_t, tokens, routes):
    hidden, width = weight_t.shape
    block = 1024
    steps = width // 2 // block
    return pl.pallas_call(
        front_kernel,
        grid_spec=pltpu.PrefetchScalarGridSpec(
            num_scalar_prefetch=1,
            grid=(steps,),
            in_specs=[
                pl.BlockSpec((hidden, block), lambda i, core: (0, (1 - core[0]) * steps + i)),
                pl.BlockSpec(tokens.shape, lambda i, core: (0, 0)),
                pl.BlockSpec(routes.shape, lambda i, core: (0, 0)),
            ],
            out_specs=[
                pl.BlockSpec((hidden, block), lambda i, core: (0, i)),
                pl.BlockSpec((256, FOLD + EXTRA), lambda i, core: (0, 0)),
            ],
            scratch_shapes=[pltpu.VMEM((PAD, tokens.shape[1]), F32), pltpu.VMEM((PAD, EXTRA), F32)],
        ),
        out_shape=(
            jax.ShapeDtypeStruct((hidden, width // 2), BF),
            jax.ShapeDtypeStruct((256, FOLD + EXTRA), BF),
        ),
        compiler_params=params(60),
        cost_estimate=pl.CostEstimate(flops=10**6, bytes_accessed=4700000, transcendentals=0),
    )(core, weight_t, tokens, routes)


def unfold_kernel(at_ref, rows_ref, out_ref):
    width = out_ref.shape[1] - EXTRA
    rows = rows_ref[...]
    r, s = iota((32, 256), 0), iota((32, 256), 1)
    for fold in range(width // FOLD):
        move = jnp.where(s == r * 8 + fold, 1.0, 0.0).astype(BF)
        piece = jnp.dot(move, rows[:, :FOLD], preferred_element_type=F32)
        out_ref[:, fold * FOLD : fold * FOLD + FOLD] = piece.astype(BF)
    move = jnp.where((s == (at_ref[0] * 2 + r // 8) * 16 + r % 8) & (r < 16), 1.0, 0.0).astype(BF)
    out_ref[:, width:] = jnp.dot(move, rows[:, FOLD:], preferred_element_type=F32).astype(BF)


def unfold(at, rows, width):
    return pl.pallas_call(
        unfold_kernel,
        in_specs=[pl.BlockSpec(memory_space=pltpu.SMEM), pl.BlockSpec(memory_space=pltpu.VMEM)],
        out_shape=jax.ShapeDtypeStruct((32, width + EXTRA), BF),
        compiler_params=params(),
        cost_estimate=pl.CostEstimate(flops=10**6, bytes_accessed=1000000, transcendentals=0),
    )(at, rows)


def choose_kernel(at_ref, *refs):
    out_ref = refs[-1]
    shape = (8 * 2 * PAD, 512)
    row, column = iota(shape, 0), iota(shape, 1)
    expert = at_ref[0] * 8 + column // 32 % 4 * 2 + column // 256
    routes = jnp.concatenate([ref[...] for ref in refs[:-1]], axis=0)
    r, s = iota((128, 256), 0), iota((128, 256), 1)
    came = (r // 8) % 2 * 128 + jnp.bitwise_xor((r // 16) % 4, at_ref[1]) * 32 + r // 64 * 8 + r % 8
    move = jnp.where(came == s, 1.0, 0.0).astype(BF)
    named = named_mask(jnp.dot(move, routes, preferred_element_type=F32), expert.astype(F32))
    r, s = iota((128, 128), 0), iota((128, 128), 1)
    lower = jnp.where((r // PAD == s // PAD) & (r > s), 1.0, 0.0)
    before = jnp.dot(lower.astype(BF), named.astype(BF), preferred_element_type=F32)
    device = row // 16 * 2 + jnp.bitwise_xor((row // 8) % 2, at_ref[2])
    fits = (before == (column % 2).astype(F32)) & (device == (column // 2) % 16)
    chosen = jnp.where(fits, named, 0.0).astype(BF)
    r, s = iota((192, 128), 0), iota((192, 128), 1)
    late = r // 64
    token = r % 8 + jnp.where(late == 0, 0, 12 - 4 * late)
    real = (late == 0) | ((token >= 8) & (token < 12))
    place = r % 64 // 8 * 16 + token // TOK * PAD + token % TOK
    move = jnp.where((place == s) & real, 1.0, 0.0).astype(BF)
    out_ref[...] = jnp.dot(move, chosen, preferred_element_type=F32).astype(BF)


def chooser(at, *runs):
    last = runs[0].shape[1] // EXTRA - 1
    return pl.pallas_call(
        choose_kernel,
        grid=(1,),
        in_specs=[pl.BlockSpec(memory_space=pltpu.SMEM)]
        + [pl.BlockSpec((value.shape[0], EXTRA), lambda i: (0, last)) for value in runs],
        out_specs=pl.BlockSpec((192, 512), lambda i: (0, 0)),
        out_shape=jax.ShapeDtypeStruct((192, 512), BF),
        compiler_params=params(),
        cost_estimate=pl.CostEstimate(flops=10**6, bytes_accessed=200000, transcendentals=0),
    )(at, *runs)


def combine_kernel(choice_ref, back_ref, out_ref):
    half = back_ref.shape[1]
    step = half // 4
    for at in range(0, half // 2, step):
        low = jnp.dot(choice_ref[...], back_ref[:, at : at + step], preferred_element_type=F32)
        high = back_ref[:, half // 2 + at : half // 2 + at + step]
        high = jnp.dot(choice_ref[...], high, preferred_element_type=F32)
        out_ref[:, at : at + step] = low[:64].astype(BF)
        out_ref[:, half // 2 + at : half // 2 + at + step] = high[:64].astype(BF)
        out_ref[:, half + at : half + at + step] = (low[64:128] + high[128:]).astype(BF)


def combined(choice, back):
    rows, half = back.shape
    return pl.pallas_call(
        combine_kernel,
        out_shape=jax.ShapeDtypeStruct((64, half + half // 2), BF),
        compiler_params=params(),
        cost_estimate=pl.CostEstimate(flops=2 * 192 * rows * half, bytes_accessed=4000000, transcendentals=0),
    )(choice, back)


def total_kernel(parts_ref, mine_ref, other_ref):
    half = mine_ref.shape[1]
    total = parts_ref[0].astype(F32)
    for source in range(1, parts_ref.shape[0]):
        total += parts_ref[source].astype(F32)
    total = total.astype(BF)
    mine_ref[...] = total[:, :half]
    r, s = iota((PAD, PAD), 0), iota((PAD, PAD), 1)

    def moved(shift, keep, value):
        move = jnp.where((s == r + shift) & keep, 1.0, 0.0).astype(BF)
        return jnp.dot(move, value, preferred_element_type=F32)

    first = moved(TOK, r < 2, total[:, :half])
    second = (r >= 2) & (r < TOK)
    rest = total[:, half:]
    rest = jnp.concatenate([moved(-2, second, rest), moved(2, second, rest)], axis=1)
    other_ref[...] = (first + rest).astype(BF)


def totalled(parts):
    half = parts.shape[2] * 2 // 3
    like = jax.ShapeDtypeStruct((PAD, half), BF)
    return pl.pallas_call(
        total_kernel,
        out_shape=(like, like),
        compiler_params=params(),
        cost_estimate=SMALL,
    )(parts)


def order_kernel(own_ref, ut_ref, out_ref):
    row, column = iota((512, 512), 0), iota((512, 512), 1)
    near = (column // 128) % 2 * 16 + (column // 32) % 4 * 4 + column // 256 * 2
    origin = column // 2 % 2 * 256 + column % 32 // 4 * 32 + jnp.bitwise_xor(own_ref[0], near) + column % 2
    move = jnp.where(row == origin, 1.0, 0.0).astype(BF)
    out_ref[...] = jnp.dot(ut_ref[...], move, preferred_element_type=F32).astype(BF)


def ordered(own, ut):
    return pl.pallas_call(
        order_kernel,
        in_specs=[pl.BlockSpec(memory_space=pltpu.SMEM), pl.BlockSpec(memory_space=pltpu.VMEM)],
        out_shape=jax.ShapeDtypeStruct(ut.shape, BF),
        compiler_params=params(),
        cost_estimate=SMALL,
    )(own, ut)


def weight_kernel(count, u_ref, *refs):
    rows = jnp.concatenate([ref[...] for ref in refs[:count]], axis=0)
    refs[-1][...] = jnp.dot(u_ref[...], rows, preferred_element_type=F32).astype(BF)


def weight_grad(u, blocks, width, block):
    hidden = u.shape[0]
    specs = [pl.BlockSpec(u.shape, lambda i: (0, 0))]
    specs += [pl.BlockSpec((value.shape[0], block), lambda i: (0, i)) for value in blocks]
    return pl.pallas_call(
        functools.partial(weight_kernel, len(blocks)),
        grid=(width // block,),
        in_specs=specs,
        out_specs=pl.BlockSpec((hidden, block), lambda i: (0, i)),
        out_shape=jax.ShapeDtypeStruct((hidden, width), BF),
        compiler_params=params(),
        cost_estimate=pl.CostEstimate(
            flops=2 * hidden * 512 * width, bytes_accessed=2 * (512 + hidden) * width, transcendentals=0
        ),
    )(u, *blocks)


def swap(value, axis):
    return lax.ppermute(value, axis, [(0, 1), (1, 0)])


def cross(value, mask):
    return lax.ppermute(value, "zl", [(i, i ^ mask) for i in range(4)])


def body(tokens, routes, up_weight, gate_pre, grad_hidden):
    place = {name: lax.axis_index(name).astype(I32) for name in AXES}
    core, zh, zl, yi = place["c"], place["zh"], place["zl"], place["yi"]
    own_arg = (yi * 16 + zl * 4 + core * 2)[None]
    at_arg = jnp.stack([zh, zl, core])
    home_arg = (place["x"] * 2 + place["yp"])[None]
    weight_t = jnp.swapaxes(up_weight, 1, 2)[0]
    hidden, width = weight_t.shape
    half = width // 2

    give, rows = front(core[None], weight_t, tokens, routes.T)
    arrived = lax.all_to_all(
        rows.reshape(16, 16, FOLD + EXTRA), FAR, split_axis=0, concat_axis=0, tiled=True
    ).reshape(256, FOLD + EXTRA)

    other_t = swap(give, "c")
    ut, u = gated(jnp.swapaxes(gate_pre, 1, 2)[0], jnp.swapaxes(grad_hidden, 1, 2)[0])
    other_u = swap(u, "c")
    terms = terms_of(core[None], u, other_u, weight_t, other_t)
    back = lax.all_to_all(
        terms.reshape(16, 32, half), PLANE, split_axis=0, concat_axis=0, tiled=True
    ).reshape(512, half)

    two = unfold(home_arg, arrived, width)
    run = jnp.concatenate([two] + [cross(two, k) for k in (1, 2, 3)], axis=0)
    other_run = swap(run, "c")
    pair = swap(run, "yi")
    u_rows = ordered(own_arg, ut)
    choice = chooser(at_arg, run, other_run)

    sums = combined(choice, back)
    parts = lax.all_to_all(
        sums.reshape(8, PAD, half + half // 2), RING, split_axis=0, concat_axis=0, tiled=True
    )

    mine, other = totalled(parts)
    other = swap(other, "c")

    pair = lax.optimization_barrier((pair, sums))[0]
    pair, other = lax.optimization_barrier((pair, other))
    rows = [run, pair, other_run, swap(pair, "c")]
    grad = weight_grad(u_rows, rows, width, 2048)

    left, right = jnp.where(core == 0, mine, other), jnp.where(core == 0, other, mine)
    grad_rows = jnp.concatenate([left, right], axis=1)[:TOK]
    return (grad_rows, jnp.swapaxes(grad[None], 1, 2))


def solution(mesh):
    fine = Mesh(mesh.devices.reshape(SIZES), AXES)
    part, column = AXES[:4], AXES[4:]
    in_specs = (
        P(AXES, None),
        P(AXES, None),
        P(part, None, column),
        P(part, None, column),
        P(part, None, column),
    )
    out_specs = (P(AXES, None), P(part, None, column))
    return jax.shard_map(body, mesh=fine, in_specs=in_specs, out_specs=out_specs, check_vma=False)
```
